256 devices in a mesh: group: 16 (over y, z_hi, core), dev: 16 (over z_lo, x).
Axes of the slice: x: 4, y: 4, z: 8 (z_hi: 2, z_lo: 4; z = z_hi * 4 + z_lo), core: 2. Of those that a mesh axis runs over, the one named last changes fastest.
Arguments:
- question_encoder_states: bfloat16 [2048, 1024], P(('group', 'dev')), may hold values from -24 to 24
- query_proj: bfloat16 [1024, 768], replicated, may hold values from -0.1875 to 0.1875
- positive_embed: bfloat16 [2048, 768], P(('group', 'dev')), may hold values from -6 to 6
- stale_index: bfloat16 [524288, 768], P(('group', 'dev')), may hold values from -6 to 6
- neg_owner: int32 [2048, 128, 1], P(('group', 'dev')), may hold values from 0 to 255; in each aligned block of 1024 rows (0 to 1023, 1024 to 2047, ..., all dimensions but the last counted through in order) at most 8 rows name the same one
- neg_row: int32 [2048, 128], P(('group', 'dev')), may hold values from 0 to 2047
- neg_count: int32 [2048], P(('group', 'dev')), may hold values from 1 to 128, 196608 in all
- slab_hidden: bfloat16 [524288, 1024], P(('group', 'dev')), may hold values from -6 to 6
- passage_projector: bfloat16 [1024, 768], P(None, 'dev'), may hold values from -0.1875 to 0.1875
Outputs:
- losses: float32 [2048], P(('group', 'dev'))
- proj_grad: float32 [1024, 768], P('dev')
- renewed_document_vectors: bfloat16 [524288, 768], P(('group', 'dev'))
The draws below stay inside these ranges and needn't reach their ends.
Inputs may be any that keep to these rules, and one draw needn't show every extreme that they name: `neg_owner`: among the 128 slots of the 8 queries of one device, no shard is named more than 8 times.
All inputs are finite; a program needn't handle non-finite values. No bound on the sum of `neg_count` on one device may be relied on, other than what follows from the above.
Results may differ from the reference program's by a relative error of at most 0.001.
Values may be sent and summed in bfloat16 or wider, within the bound.
A program may use at most 64 MiB of HBM per device.

```python
import math
import jax
import jax.numpy as jnp
import numpy as np
from jax import lax

D = 1024
E = 768
NEG = 128
Q_DEV = 8
IDX_DEV = 2048
QUERIES = 2048
PASSAGES = 524288
CAP = 8
DEVICES = 256


def with_ends(array, stream_key, low, top_value):
    index_at = [jax.random.randint(jax.random.fold_in(stream_key, axis), (), 0, length) for axis, length in enumerate(array.shape)]
    widest = array.shape.index(max(array.shape))
    neighbour = index_at[:widest] + [(index_at[widest] + 1) % array.shape[widest]] + index_at[widest + 1:]
    return array.at[tuple(index_at)].set(low).at[tuple(neighbour)].set(top_value)


def spiked(result, own_key, source, target, blocks, factor):
    owner, partner = [(jnp.arange(result.shape[axis_at]) // (result.shape[axis_at] // blocks)).reshape([-1 if axis == axis_at else 1 for axis in range(result.ndim)]) for axis_at in (source, target)]
    chosen = jax.random.permutation(own_key, blocks)[partner]
    strong = (owner == chosen) | (owner == (partner + blocks // 2) % blocks)
    return jnp.where(strong, factor * result, result)


def shard_levels(stream_key, extent, pieces, low, top_value):
    def one(dim, shards_of):
        steps = jax.random.uniform(jax.random.fold_in(jax.random.fold_in(stream_key, 6), dim), (shards_of,), jnp.float32, low / len(pieces), top_value / len(pieces))
        return jnp.repeat(jnp.exp(steps), extent[dim] // shards_of).reshape((-1,) + (1,) * (len(extent) - dim - 1))

    gain = one(*pieces[0])
    for cut in pieces[1:]:
        gain = gain * one(*cut)
    return gain


def split_up(count, total, reach, skew):
    portions = [(1 << 20) // math.isqrt(grade ** skew) + 1 for grade in range(2, count + 1)]
    surplus, counts = total - reach - (count - 1), [1] * (count - 1)
    while surplus > 0:
        free = [i for i in range(count - 1) if counts[i] < reach]
        whole, left = sum([portions[i] for i in free]), surplus
        for i in free:
            extra = min(reach - counts[i], max(1, left * portions[i] // whole), surplus)
            counts[i] = counts[i] + extra
            surplus = surplus - extra
    return np.array([reach] + counts)


def uneven(key, count, total, reach, skew):
    if count == 2:
        one = jax.random.randint(key, (), max(1, total - reach), min(reach, total - 1) + 1)
        return jnp.stack([one, total - one])
    tallies = jnp.asarray(split_up(count, total, reach, skew), jnp.int32)
    couples = (count - 1) // 2
    giver, sink = tallies[1:1 + 2 * couples:2], tallies[2:2 + 2 * couples:2]
    room = jnp.minimum(giver - 1, reach - sink)
    moved = jax.random.randint(jax.random.fold_in(key, 1), (couples,), 0, 1 << 20) % (room + 1)
    tallies = tallies.at[1:1 + 2 * couples:2].set(giver - moved).at[2:2 + 2 * couples:2].set(sink + moved)
    return tallies[jax.random.permutation(jax.random.fold_in(key, 2), count)]


def routed_block(key, own, number, rows, amount, top, reach, lean):
    order = jax.random.permutation(key, amount)
    heavy_load, ordinary = load_shares(amount, rows * top, reach, lean, True), load_shares(amount, rows * top, reach, lean, False)
    places = jnp.arange(amount)

    def named(sizes, rotation):
        used = int((sizes > 0).sum())
        fixed = max(1, used // 4)
        moved = fixed + (places - fixed + rotation * (used - fixed)) % max(1, amount - fixed)
        return jnp.zeros((amount,), jnp.int32).at[order[jnp.where(places < fixed, places, moved)]].set(jnp.asarray(sizes, jnp.int32))

    sizes = jnp.where(number % 4 == 0, named(heavy_load, number // 4), named(ordinary, number - number // 4 - 1))
    mixed = jax.random.permutation(jax.random.fold_in(own, 3), amount)
    giver, sink = mixed[0:amount // 2 * 2:2], mixed[1:amount // 2 * 2:2]
    slack = jnp.minimum(sizes[giver] - 1, reach - sizes[sink]) // 2
    slack = jnp.where((giver == order[0]) | (sink == order[0]) | (sizes[sink] == 0), 0, jnp.maximum(slack, 0))
    moved = jax.random.randint(jax.random.fold_in(own, 4), (amount // 2,), 0, 1 << 20) % (slack + 1)
    sizes = sizes.at[giver].add(-moved).at[sink].add(moved)
    members = jnp.searchsorted(jnp.cumsum(sizes), jnp.arange(rows * top), side="right").astype(jnp.int32)
    table = members.reshape(top, rows).T
    table = table[jax.random.permutation(jax.random.fold_in(own, 1), rows)]
    rotation = jax.random.randint(jax.random.fold_in(own, 2), (rows, 1), 0, top)
    return jnp.take_along_axis(table, (jnp.arange(top)[None, :] + rotation) % top, axis=1)


def load_shares(number_of, total, limit, slope, full):
    portions = [(1 << 20) // math.isqrt(standing ** slope) + 1 for standing in range(1, number_of + 1)]
    largest = limit if full else min(limit, max(-(-total // number_of), total * portions[0] // sum(portions)))
    least = 1 if total - largest >= number_of - 1 else 0
    holding, spare = [largest] + [least] * (number_of - 1), total - largest - least * (number_of - 1)
    while spare > 0:
        free = [i for i in range(1, number_of) if holding[i] < largest] or [i for i in range(1, number_of) if holding[i] < limit]
        pool, remaining = sum([portions[i] for i in free]), spare
        for i in free:
            more = min(limit - holding[i], max(1, remaining * portions[i] // pool), spare)
            holding[i] = holding[i] + more
            spare = spare - more
    return np.array(holding)


def centred(own_key, shape, width, limit, pieces=(), dtype=jnp.bfloat16):
    entries = jax.random.normal(own_key, shape, jnp.float32) * width
    if len(pieces) > 0:
        entries = shard_levels(own_key, shape, pieces, -0.22, 0.18) * entries
    return jnp.clip(entries, min=-limit, max=limit).astype(dtype)


def noise_with(own_key, dims, scale, most, split, heavy, held_as=jnp.bfloat16):
    array = scale * jax.random.normal(own_key, dims, jnp.float32)
    if split:
        array = array * shard_levels(own_key, dims, split, -0.22, 0.18)
    return jnp.clip(spiked(array, jax.random.fold_in(own_key, 3), *heavy), -most, most).astype(held_as)


def setup_inputs(seed: int = 0) -> dict:
    key_of = jax.random.split(jax.random.key(seed), 10)
    question_encoder_states = noise_with(key_of[0], (QUERIES, D), 1.0, 24.0, ((0, 256),), (0, 1, 256, 6.0))
    query_proj = centred(key_of[1], (D, E), D ** -0.5, 0.1875)
    positive_embed = centred(key_of[2], (QUERIES, E), 1.0, 6.0, ((0, 256),))
    stale_index = centred(key_of[3], (PASSAGES, E), 1.0, 6.0, ((0, 256),))
    neg_owner_keys = jax.random.split(jax.random.fold_in(key_of[4], 1), QUERIES * NEG // (Q_DEV * NEG))
    neg_owner_turns = jax.random.permutation(jax.random.fold_in(key_of[4], 3), QUERIES * NEG // (Q_DEV * NEG))
    neg_owner = jax.vmap(lambda own, number: routed_block(jax.random.fold_in(key_of[4], 2), own, number, Q_DEV * NEG, DEVICES, 1, CAP, 2))(neg_owner_keys, neg_owner_turns).reshape((QUERIES, NEG, 1))
    neg_row = with_ends(jax.random.randint(key_of[5], (QUERIES, NEG), 0, IDX_DEV), jax.random.fold_in(key_of[5], 1), 0, IDX_DEV - 1).astype(jnp.int32)
    neg_count = uneven(key_of[6], QUERIES, 3 * NEG * QUERIES // 4, NEG, 2).astype(jnp.int32)
    slab_hidden = centred(key_of[7], (PASSAGES, D), 1.0, 6.0, ((0, 256),))
    passage_projector = centred(key_of[8], (D, E), D ** -0.5, 0.1875, ((1, 16),))
    return dict(question_encoder_states=question_encoder_states, query_proj=query_proj, positive_embed=positive_embed, stale_index=stale_index, neg_owner=neg_owner, neg_row=neg_row, neg_count=neg_count, slab_hidden=slab_hidden, passage_projector=passage_projector)


epsilon = 1e-06
sharpness_divisor = 0.05

def normalized_rows(values):
    return values * lax.rsqrt(lax.optimization_barrier(jnp.mean(values * values, axis=-1, keepdims=True)) + epsilon)

def query_loss(question_vector_raw_length, positive_passage, fetched, live_count):
    query_unit = normalized_rows(question_vector_raw_length)
    pos_unit = normalized_rows(positive_passage.astype(jnp.float32))
    neg_unit = normalized_rows(fetched.astype(jnp.float32))
    similarity_multiplier = 1.0 / (question_vector_raw_length.shape[-1] * sharpness_divisor)
    pos_score = lax.optimization_barrier(jnp.sum(query_unit * pos_unit, axis=-1)) * similarity_multiplier
    neg_score = jnp.einsum('be,bne->bn', query_unit, neg_unit, precision=lax.Precision.HIGHEST) * similarity_multiplier
    candidate_position_range = lax.broadcasted_iota(jnp.int32, neg_score.shape, 1)
    live_mask = candidate_position_range < live_count[:, None]
    partition = jnp.exp(pos_score) + lax.optimization_barrier(jnp.sum(jnp.where(live_mask, jnp.exp(neg_score), 0.0), axis=-1))
    return jnp.log(partition) - pos_score

def reference(question_encoder_states, query_proj, positive_embed, stale_index, neg_owner, neg_row, neg_count, slab_hidden, passage_projector):

    def one_block(block_args):
        hidden_rows, positive_passage, owner_ids, row_ids, live_count = block_args
        question_vector_raw_length = jnp.dot(hidden_rows, query_proj, preferred_element_type=jnp.float32)
        passage_ids = (owner_ids[..., 0].astype(jnp.int32) * IDX_DEV + row_ids.astype(jnp.int32)).astype(jnp.int32)
        fetched = jnp.take(stale_index, passage_ids.reshape(-1), axis=0).reshape(passage_ids.shape + (stale_index.shape[1],))
        block_loss, backward_pass = jax.vjp(lambda query_vec: query_loss(query_vec, positive_passage, fetched, live_count), question_vector_raw_length)
        pull_back, = backward_pass(jnp.ones_like(block_loss))
        return (block_loss, pull_back)
    block_loss, pull_back = lax.map(one_block, (question_encoder_states.reshape(DEVICES, Q_DEV, D), positive_embed.reshape(DEVICES, Q_DEV, E), neg_owner.reshape(DEVICES, Q_DEV, NEG, 1), neg_row.reshape(DEVICES, Q_DEV, NEG), neg_count.reshape(DEVICES, Q_DEV)))
    losses = block_loss.reshape(QUERIES)
    proj_grad = jnp.dot(question_encoder_states.astype(jnp.float32).T, pull_back.reshape(QUERIES, E), precision=lax.Precision.HIGHEST)

    def encode_block(slab_rows):
        return jnp.dot(slab_rows, passage_projector, preferred_element_type=jnp.float32).astype(jnp.bfloat16)
    renewed_document_vectors = lax.map(encode_block, slab_hidden.reshape(DEVICES, IDX_DEV, D)).reshape(PASSAGES, E)
    return (losses, proj_grad, renewed_document_vectors)
```

```python
import jax
import jax.numpy as jnp
from jax import lax
from jax.experimental import pallas as pl
from jax.experimental.pallas import tpu as pltpu
from jax.sharding import PartitionSpec as P

MESH = pl.DeviceIdType.MESH
F32 = jnp.float32
BF16 = jnp.bfloat16
EPS = 1e-06
DIV = 0.05
E = 768
D = 1024
SCALE = 1.0 / (E * DIV)
NX, NY, NZ = 4, 4, 8
X_FIRST = (True, True, False, True, False, False)


def iota(shape, dim):
    return lax.broadcasted_iota(jnp.int32, shape, dim)


def nt(a, b):
    return lax.dot_general(a, b, (((1,), (1,)), ((), ())), preferred_element_type=F32)


def tn(a, b):
    return lax.dot_general(a, b, (((0,), (0,)), ((), ())), preferred_element_type=F32)


def device_of(x, y, z, c):
    return ((y * 2 + z // 4) * 2 + c, lax.rem(z, 4) * 4 + x)


def body(
    h_ref, req_ref, pos_ref, pt_ref, wq_hbm, idx_hbm, slab_hbm,
    loss_ref, grad_ref, ren_hbm,
    wq, idx, slab, ren, local_sem,
    buf_a, buf_b, h_t, tab, tab_z, tab_y, tab_j, tab_r,
    pbuf, rows, ghat, gmat, zbuf, zrecv, zsum, zcol,
    tt, tcore, tsum, r1, p1, r2, p2, r3, fin,
    ssem, rsem,
):
    g = lax.axis_index("group")
    d = lax.axis_index("dev")
    x = lax.rem(d, 4)
    c = lax.rem(g, 2)
    y = g // 4
    z = lax.rem(g // 2, 2) * 4 + d // 4
    blk = x * 2 + c

    def near(dx, dy, dz, dc):
        return (
            lax.rem(x + dx + NX, NX),
            lax.rem(y + dy + NY, NY),
            lax.rem(z + dz + NZ, NZ),
            lax.rem(c + dc, 2),
        )

    used = [0]
    sent = []

    def copy(src, dst, at):
        n = used[0]
        used[0] = n + 1
        r = pltpu.make_async_remote_copy(
            src_ref=src, dst_ref=dst, send_sem=ssem.at[n], recv_sem=rsem.at[n],
            device_id=device_of(*at), device_id_type=MESH,
        )
        r.start()
        sent.append(r)
        return r

    loads = []
    for n, (src, dst) in enumerate(((wq_hbm, wq), (idx_hbm, idx), (slab_hbm, slab))):
        load = pltpu.make_async_copy(src, dst, local_sem.at[n])
        load.start()
        loads.append(load)

    peers = [(0, 0, i, 0) for i in range(1, NZ)]
    peers += [(i, j, 0, 0) for i in range(NX) for j in range(NY) if i or j]
    peers += [(i, 0, 0, 1) for i in range(NX)]
    peers += [(0, j, 0, 1) for j in range(1, NY)]
    barrier = pltpu.get_barrier_semaphore()
    for p in peers:
        pl.semaphore_signal(barrier, inc=1, device_id=device_of(*near(*p)), device_id_type=MESH)

    h32 = h_ref[...].astype(F32)
    buf_a[x, c, y, z] = jnp.concatenate([h32[:, 0:256], h32[:, 256:512]], axis=0).astype(BF16)
    buf_b[x, c, y, z] = jnp.concatenate([h32[:, 512:768], h32[:, 768:1024]], axis=0).astype(BF16)
    pbuf[c, lax.rem(z, 4), x] = pt_ref[c]
    pl.semaphore_wait(barrier, len(peers))

    z_a = [copy(buf_a.at[x, c, y, z], buf_a.at[x, c, y, z], near(0, 0, o, 0)) for o in range(1, NZ)]
    z_b = [copy(buf_b.at[x, c, y, z], buf_b.at[x, c, y, z], near(0, 0, o, 0)) for o in range(1, NZ)]
    zl = lax.rem(z, 4)
    p_x = [copy(pbuf.at[c, zl, x], pbuf.at[c, zl, x], near(o, 0, 0, 0)) for o in range(1, NX)]

    lane = iota((128, 128), 1)
    kind, place = lane % 16, lane // 16
    lower = (iota((128, 128), 0) > lane).astype(F32).astype(BF16)
    owner_lane = iota((128, 256), 1).astype(F32)
    carry = jnp.zeros((1, 256), F32)
    table = jnp.zeros((256, 128), F32)
    for i in range(8):
        code = req_ref[:, i:i + 1]
        row = req_ref[:, 8 + i:9 + i]
        hit = (code == owner_lane).astype(F32)
        before = jnp.dot(lower, hit.astype(BF16), preferred_element_type=F32) + carry
        rank = jnp.sum(hit * before, axis=1, keepdims=True)
        carry = carry + jnp.sum(hit, axis=0, keepdims=True)
        high = jnp.floor(row * (1.0 / 16.0))
        low = row - 16.0 * high
        value = jnp.where(kind == 0, high, jnp.where(kind == 1, low, jnp.where(kind == 2, i + 1.0, 0.0)))
        value = jnp.where(rank == place.astype(F32), value, 0.0)
        table = table + tn(hit.astype(BF16), value.astype(BF16))
    tab[...] = table.reshape(NZ, NY, 8, 128)

    t_z = [
        copy(tab.at[near(0, 0, o, 0)[2]], tab_z.at[z], near(0, 0, o, 0)) for o in range(1, NZ)
    ]
    tab_z[z] = tab[z]

    def spread(buf, waits, mid, last):
        for w in waits:
            w.wait_recv()
        mids = [copy(buf.at[x, c, y], buf.at[x, c, y], near(*mid(o))) for o in range(1, 4)]
        lasts = [copy(buf.at[x, c, y], buf.at[x, c, y], near(*last(o))) for o in range(1, 4)]
        cores = [copy(buf.at[x, c, y], buf.at[x, c, y], near(0, 0, 0, 1))]
        return mids, lasts, cores

    def along_x(o):
        return (o, 0, 0, 0)

    def along_y(o):
        return (0, o, 0, 0)

    mid_a, last_a, core_a = spread(buf_a, z_a, along_y, along_x)
    mid_b, last_b, core_b = spread(buf_b, z_b, along_x, along_y)

    for w in t_z:
        w.wait_recv()
    t_y = [
        copy(tab_z.at[:, near(0, o, 0, 0)[1]], tab_y.at[y], near(0, o, 0, 0)) for o in range(1, NY)
    ]
    tab_y[y] = tab_z[:, y]

    for w in p_x:
        w.wait_recv()
    p_z = [copy(pbuf.at[c, zl], pbuf.at[c, zl], near(0, 0, o, 0)) for o in (1, 7)]
    p_z += [copy(pbuf.at[c, zl, 0:2], pbuf.at[c, zl, 0:2], near(0, 0, 2, 0))]
    p_z += [copy(pbuf.at[c, zl, 2:4], pbuf.at[c, zl, 2:4], near(0, 0, 6, 0))]

    for o in range(1, 4):
        mid_a[o - 1].wait_recv()
        grp = buf_a.at[x, c, lax.rem(y - o + NY, NY)]
        last_a += [copy(grp, grp, near(*along_x(q))) for q in range(1, 4)]
        core_a.append(copy(grp, grp, near(0, 0, 0, 1)))
        mid_b[o - 1].wait_recv()
        grp = buf_b.at[lax.rem(x - o + NX, NX), c, y]
        last_b += [copy(grp, grp, near(*along_y(q))) for q in range(1, 4)]
        core_b.append(copy(grp, grp, near(0, 0, 0, 1)))

    for w in t_y:
        w.wait_recv()
    tab_j[...] = jnp.swapaxes(tab_y[...].reshape(NY * NZ, 8, 128), 0, 1)
    t_j = []
    for o in range(NX):
        for k in range(2):
            if o or k:
                at = near(o, 0, 0, k)
                t_j.append(copy(tab_j.at[at[0] * 2 + at[3]], tab_r.at[blk], at))
    tab_r[blk] = tab_j[blk]

    loads[0].wait()
    q_own = jnp.dot(h_ref[...], wq[...], preferred_element_type=F32)
    rq_own = lax.rsqrt(jnp.mean(q_own * q_own, axis=1, keepdims=True) + EPS)
    u_own = q_own * rq_own
    pos = pos_ref[...].astype(F32)
    pos = pos * lax.rsqrt(jnp.mean(pos * pos, axis=1, keepdims=True) + EPS)
    pos_dot = jnp.sum(u_own * pos, axis=1, keepdims=True)
    pos_score = pos_dot * SCALE
    pos_exp = jnp.exp(pos_score)
    pos_dir = (pos - u_own * (pos_dot * (1.0 / E))) * (rq_own * SCALE)

    loads[1].wait()
    for w in t_j:
        w.wait_recv()
    src, out = iota((128, 2048), 0), iota((128, 2048), 1)
    slot, want_q = out // 256, (out // 128) % 2
    weight = jnp.where(src % 16 == 0, 16.0, 1.0)
    kept = jnp.where(want_q == 0, jnp.where(src % 16 < 2, weight, 0.0), jnp.where(src % 16 == 2, 1.0, 0.0))
    expand = jnp.where(src // 16 == slot, kept, 0.0).astype(BF16)

    def columns_of(b):
        wide = jnp.dot(tab_r[b].astype(BF16), expand, preferred_element_type=F32)
        row = jnp.concatenate([wide[:, k * 256:k * 256 + 128] for k in range(8)], axis=0)
        qry = jnp.concatenate([wide[:, k * 256 + 128:k * 256 + 256] for k in range(8)], axis=0)
        return row, qry

    lane_f = iota((256, 128), 1).astype(F32)

    def pick(b, _):
        row, _q = columns_of(b)
        hot = jnp.concatenate(
            [(row == lane_f + 128.0 * t).astype(F32).astype(BF16) for t in range(16)], axis=1
        )
        rows[b] = jnp.dot(hot, idx[...], preferred_element_type=F32).astype(BF16)
        return 0

    lax.fori_loop(0, 8, pick, 0)

    for j in range(4):
        for q in range(1, 4):
            last_a[j * 3 + q - 1].wait_recv()
            grp = buf_a.at[lax.rem(x - q + NX, NX), c, lax.rem(y - j + NY, NY)]
            core_a.append(copy(grp, grp, near(0, 0, 0, 1)))
            last_b[j * 3 + q - 1].wait_recv()
            grp = buf_b.at[lax.rem(x - j + NX, NX), c, lax.rem(y - q + NY, NY)]
            core_b.append(copy(grp, grp, near(0, 0, 0, 1)))
    for w in p_z:
        w.wait_recv()
    p_c = copy(pbuf.at[c], pbuf.at[c], near(0, 0, 0, 1))
    for w in core_a + core_b:
        w.wait_recv()

    group_of = (iota((256, 256), 0) % 32 * 8 - 1).astype(F32)
    query_lane = iota((256, 256), 1).astype(F32)

    def score(b, _):
        sides = []
        xb, cb = b // 2, lax.rem(b, 2)
        for buf in (buf_a, buf_b):
            part = buf[xb, cb].astype(F32).reshape(32, 16, 256)
            sides += [part[:, 0:8].reshape(256, 256), part[:, 8:16].reshape(256, 256)]
        hb = jnp.concatenate([s.astype(BF16) for s in sides], axis=1)
        for n, s in enumerate(sides):
            h_t[pl.ds(n * 256, 256), pl.ds(pl.multiple_of(b * 256, 256), 256)] = s.T.astype(BF16)
        q = jnp.dot(hb, wq[...], preferred_element_type=F32)
        rq = lax.rsqrt(jnp.mean(q * q, axis=1, keepdims=True) + EPS)
        u = q * rq
        u_hi = u.astype(BF16)
        u_lo = (u - u_hi.astype(F32)).astype(BF16)
        r = rows[b]
        r32 = r.astype(F32)
        rr = lax.rsqrt(jnp.mean(r32 * r32, axis=1, keepdims=True) + EPS)
        s = (nt(r, u_hi) + nt(r, u_lo)) * (rr * SCALE)
        _row, qry = columns_of(b)
        qry = jnp.concatenate([qry, qry], axis=1)
        live = (qry > 0.5) & (group_of + qry == query_lane)
        e = jnp.where(live, jnp.exp(s), 0.0)
        zr = jnp.sum(e, axis=0, keepdims=True)
        zbuf[pl.ds(b * 2, 1), :] = zr[:, 0:128]
        zbuf[pl.ds(b * 2 + 1, 1), :] = zr[:, 128:256]
        gb = tn((e * rr).astype(BF16), r)
        gb = gb - u * (jnp.sum(u * gb, axis=1, keepdims=True) * (1.0 / E))
        ghat[pl.ds(pl.multiple_of(b * 256, 256), 256), :] = gb * (rq * SCALE)
        return 0

    lax.fori_loop(0, 8, score, 0)

    first = (lax.rem(y, 2) * 8 + z) * 8
    sub, ln = iota((8, 128), 0), iota((8, 128), 1)
    mine = jnp.sum(jnp.where(ln == first + sub, pos_exp, 0.0), axis=0, keepdims=True)
    zbuf[...] = zbuf[...] + jnp.where(iota((16, 128), 0) == blk * 2 + y // 2, mine, 0.0)

    def half(n):
        return pl.ds(pl.multiple_of(n * 8, 8), 8)

    def encode(lo, hi):
        def step(n, _):
            at = pl.ds(pl.multiple_of(n * 256, 256), 256)
            s = slab[at, :]
            p0 = pbuf[0].reshape(E, 512)
            p1_ = pbuf[1].reshape(E, 512)
            ren[at, :] = (nt(s[:, 0:512], p0) + nt(s[:, 512:1024], p1_)).astype(BF16)
            return 0

        lax.fori_loop(lo, hi, step, 0)

    w = copy(zbuf.at[half(1 - c)], zrecv.at[0], near(0, 0, 0, 1))
    loads[2].wait()
    p_c.wait_recv()
    encode(0, 1)
    w.wait_recv()
    zsum[0] = zbuf[half(c), :] + zrecv[0]
    ws = []
    for i in range(NX):
        for j in range(NY):
            if i or j:
                ws.append(copy(zsum.at[0], zrecv.at[1 + len(ws)], near(i, j, 0, 0)))
    encode(1, 4)
    total = zsum[0]
    for n, w in enumerate(ws):
        w.wait_recv()
        total = total + zrecv[1 + n]
    zsum[1] = total
    ws = [copy(zsum.at[1], zrecv.at[15 + o], near(0, 0, o, 0)) for o in range(1, NZ)]
    encode(4, 7)
    for n, w in enumerate(ws):
        w.wait_recv()
        total = total + zrecv[16 + n]
    zsum[2] = total
    w = copy(zsum.at[2], zrecv.at[23], near(0, 0, 0, 1))
    encode(7, 8)
    w.wait_recv()
    out_copy = pltpu.make_async_copy(ren, ren_hbm, local_sem.at[3])
    out_copy.start()
    other = zrecv[23]
    top = jnp.where(c == 0, total, other)
    bottom = jnp.where(c == 0, other, total)
    padded = jnp.concatenate([top, bottom, jnp.ones((112, 128), F32)], axis=0)
    turned = padded.T
    for t in range(16):
        zcol[pl.ds(t * 128, 128), :] = jnp.broadcast_to(turned[:, t:t + 1], (128, 128))

    own = pl.ds(pl.multiple_of((blk * 32 + y * 8 + z) * 8, 8), 8)
    z_own = zcol[own, :][:, 0:1]
    loss_ref[...] = jnp.broadcast_to(jnp.log(z_own) - pos_score, (8, 128))
    ghat[own, :] = ghat[own, :] + pos_dir * (pos_exp - z_own)
    own_rows = ghat[own, :] / z_own
    own_low = own_rows - own_rows.astype(BF16).astype(F32)
    own_low = jnp.concatenate([own_low, jnp.zeros_like(own_low)], axis=0).astype(BF16)
    h_pad = jnp.concatenate([h32, jnp.zeros_like(h32)], axis=0)

    def rescale(b, _):
        at = pl.ds(pl.multiple_of(b * 128, 128), 128)
        gmat[at, :] = (ghat[at, :] / zcol[at, :][:, 0:1]).astype(BF16)
        return 0

    lax.fori_loop(0, 16, rescale, 0)

    t_c = []
    for n in range(4):
        val = jnp.dot(h_t[pl.ds(n * 256, 256), :], gmat[...], preferred_element_type=F32)
        val = val + tn(h_pad[:, n * 256:(n + 1) * 256].astype(BF16), own_low)
        for t in range(6):
            tile = val[:, t * 128:(t + 1) * 128].reshape(4, 4, 16, 128)
            if X_FIRST[t]:
                tt[t, n] = tile
            else:
                for a in range(4):
                    for b in range(4):
                        tt[t, n, a, b] = tile[b, a]
        t_c.append(
            copy(tt.at[pl.ds((1 - c) * 3, 3), n], tcore.at[n], near(0, 0, 0, 1))
        )

    unit_x = [jnp.int32(1), 1 - c, jnp.int32(0)]
    first_at = [x * f + y * (1 - f) for f in unit_x]
    second_at = [y * f + x * (1 - f) for f in unit_x]
    ph1 = []
    for n in range(4):
        t_c[n].wait_recv()
        for u in range(3):
            tsum[u, n] = tt[c * 3 + u, n] + tcore[n, u]
            f = unit_x[u]
            for o in range(1, 4):
                to = lax.rem(first_at[u] + o, 4)
                ph1.append(
                    copy(tsum.at[u, n, to], r1.at[u, o - 1, n], near(o * f, o * (1 - f), 0, 0))
                )
    for u in range(3):
        for n in range(4):
            for o in range(1, 4):
                ph1[n * 9 + u * 3 + o - 1].wait_recv()
        p1[u] = tsum[u, :, first_at[u]] + r1[u, 0] + r1[u, 1] + r1[u, 2]
    ph2 = []
    for u in range(3):
        f = unit_x[u]
        for o in range(1, 4):
            to = lax.rem(second_at[u] + o, 4)
            ph2.append(copy(p1.at[u, :, to], r2.at[u, o - 1], near(o * (1 - f), o * f, 0, 0)))
    for u in range(3):
        for o in range(1, 4):
            ph2[u * 3 + o - 1].wait_recv()
        p2[:, u] = p1[u, :, second_at[u]] + r2[u, 0] + r2[u, 1] + r2[u, 2]
    ph3 = []
    for o in range(1, NZ):
        to = near(0, 0, o, 0)
        ph3.append(copy(p2.at[lax.rem(to[2], 4)], r3.at[o - 1], to))
    done = p2[zl]
    for o in range(1, NZ):
        ph3[o - 1].wait_recv()
        done = done + r3[o - 1]
    fin[y, c] = done
    ph4 = []
    for o in range(NY):
        for k in range(2):
            if o or k:
                ph4.append(copy(fin.at[y, c], fin.at[y, c], near(0, o, 0, k)))
    for w in ph4:
        w.wait_recv()
    for j in range(NY):
        for n in range(2):
            for u in range(3):
                grad_ref[pl.ds(j * 16, 16), pl.ds(n * 384 + u * 128, 128)] = fin[j, n, u]
    for w in sent:
        w.wait_send()
    out_copy.wait()


COPIES = 256


def local(
    question_encoder_states,
    query_proj,
    positive_embed,
    stale_index,
    neg_owner,
    neg_row,
    neg_count,
    slab_hidden,
    passage_projector,
):
    owner = neg_owner[..., 0]
    og, od = owner // 16, owner % 16
    oz = (og // 2) % 2 * 4 + od // 4
    code = (oz * 4 + og // 4) * 8 + od % 4 * 2 + og % 2
    live = iota(neg_row.shape, 1) < neg_count[:, None]
    code = jnp.where(live, code, -1)
    req = jnp.concatenate([code, neg_row], axis=0).astype(F32).T
    pt = jnp.transpose(passage_projector.reshape(2, 512, 48), (0, 2, 1))
    vmem = pl.BlockSpec(memory_space=pltpu.VMEM)
    hbm = pl.BlockSpec(memory_space=pl.ANY)
    V = pltpu.VMEM
    scratch = [
        V((D, E), BF16), V((2048, E), BF16), V((2048, D), BF16), V((2048, E), BF16),
        pltpu.SemaphoreType.DMA((4,)),
        V((NX, 2, NY, NZ, 16, 256), BF16), V((NX, 2, NY, NZ, 16, 256), BF16),
        V((D, 2048), BF16),
        V((NZ, NY, 8, 128), F32), V((NZ, NY, 8, 128), F32), V((NY, NZ, 8, 128), F32),
        V((8, NY * NZ, 128), F32), V((8, NY * NZ, 128), F32),
        V((2, 4, 4, 48, 512), BF16), V((8, 256, E), BF16),
        V((2048, E), F32), V((2048, E), BF16),
        V((16, 128), F32), V((24, 8, 128), F32), V((3, 8, 128), F32), V((2048, 128), F32),
        V((6, 4, 4, 4, 16, 128), F32), V((4, 3, 4, 4, 16, 128), F32),
        V((3, 4, 4, 4, 16, 128), F32),
        V((3, 3, 4, 4, 16, 128), F32), V((3, 4, 4, 16, 128), F32),
        V((3, 3, 4, 16, 128), F32), V((4, 3, 16, 128), F32),
        V((NZ - 1, 3, 16, 128), F32), V((NY, 2, 3, 16, 128), F32),
        pltpu.SemaphoreType.DMA((COPIES,)), pltpu.SemaphoreType.DMA((COPIES,)),
    ]
    losses, grad, renewed = pl.pallas_call(
        body,
        out_shape=(
            jax.ShapeDtypeStruct((8, 128), F32),
            jax.ShapeDtypeStruct((64, E), F32),
            jax.ShapeDtypeStruct((2048, E), BF16),
        ),
        in_specs=[vmem, vmem, vmem, vmem, hbm, hbm, hbm],
        out_specs=(vmem, vmem, hbm),
        scratch_shapes=scratch,
        compiler_params=pltpu.CompilerParams(
            collective_id=0, has_side_effects=True, vmem_limit_bytes=62 * 2**20
        ),
        cost_estimate=pl.CostEstimate(
            flops=30 * 10**9, bytes_accessed=16 * 2**20, transcendentals=2**20
        ),
    )(question_encoder_states, req, positive_embed, pt, query_proj, stale_index, slab_hidden)
    return losses[:, 0], grad, renewed


def solution(mesh):
    rows = P(("group", "dev"), None)
    in_specs = (
        rows, P(), rows, rows, P(("group", "dev"), None, None), rows,
        P(("group", "dev")), rows, P(None, "dev"),
    )
    out_specs = (P(("group", "dev")), P("dev", None), rows)
    return jax.shard_map(local, mesh=mesh, in_specs=in_specs, out_specs=out_specs, check_vma=False)
```

```python
import jax
import jax.numpy as jnp
from jax import lax
from jax.experimental import pallas as pl
from jax.experimental.pallas import tpu as pltpu
from jax.sharding import PartitionSpec as P

MESH = pl.DeviceIdType.MESH
F32 = jnp.float32
BF16 = jnp.bfloat16
EPS = 1e-06
DIV = 0.05
E = 768
D = 1024
SCALE = 1.0 / (E * DIV)
NX, NY, NZ = 4, 4, 8
X_FIRST = (True, True, False, True, False, False)


def iota(shape, dim):
    return lax.broadcasted_iota(jnp.int32, shape, dim)


def nt(a, b):
    return lax.dot_general(a, b, (((1,), (1,)), ((), ())), preferred_element_type=F32)


def tn(a, b):
    return lax.dot_general(a, b, (((0,), (0,)), ((), ())), preferred_element_type=F32)


def device_of(x, y, z, c):
    return ((y * 2 + z // 4) * 2 + c, lax.rem(z, 4) * 4 + x)


def body(
    h_ref, owner_ref, row_ref, count_ref, pos_ref, pt_ref, wq_hbm, idx_hbm, slab_hbm,
    loss_ref, grad_ref, ren_hbm,
    wq, idx, slab, ren, local_sem,
    buf_a, buf_b, h_t, tab, tab_y, tab_j, tab_r,
    pbuf, rows, norm, u_two, u_scale, ghat, gmat, zbuf, zrecv, zsum, zcol,
    tt, tcore, tsum, r1, p1, r2, p2, r3, fin,
    ssem, rsem,
):
    g = lax.axis_index("group")
    d = lax.axis_index("dev")
    x = lax.rem(d, 4)
    c = lax.rem(g, 2)
    y = g // 4
    zl = d // 4
    z = lax.rem(g // 2, 2) * 4 + zl

    def near(dx, dy, dz, dc):
        return (
            lax.rem(x + dx + NX, NX),
            lax.rem(y + dy + NY, NY),
            lax.rem(z + dz + NZ, NZ),
            lax.rem(c + dc, 2),
        )

    used_s, used_r, sends = [0], [0], []

    def send_sem(ref):
        n = used_s[0]
        used_s[0] = n + 1
        sends.append((ssem.at[n], ref))
        return ssem.at[n]

    def recv_sem():
        n = used_r[0]
        used_r[0] = n + 1
        return rsem.at[n]

    def await_bytes(sem, ref):
        pltpu.make_async_copy(ref, ref, sem).wait()

    def copy(src, dst, at, s_sem, r_sem):
        pltpu.make_async_remote_copy(
            src_ref=src, dst_ref=dst, send_sem=s_sem, recv_sem=r_sem,
            device_id=device_of(*at), device_id_type=MESH,
        ).start()

    peers = [(0, 0, i, 0) for i in range(1, NZ)]
    peers += [(i, j, 0, 0) for i in range(NX) for j in range(NY) if i or j]
    peers += [(0, 0, i, 1) for i in range(NZ)]
    peers += [(0, j, 0, 1) for j in range(1, NY)]
    barrier = pltpu.get_barrier_semaphore()
    for p in peers:
        pl.semaphore_signal(barrier, inc=1, device_id=device_of(*near(*p)), device_id_type=MESH)

    h32 = h_ref[...].astype(F32)
    buf_a[x, c, y, z] = jnp.concatenate([h32[:, 0:256], h32[:, 256:512]], axis=0).astype(BF16)
    buf_b[x, c, y, z] = jnp.concatenate([h32[:, 512:768], h32[:, 768:1024]], axis=0).astype(BF16)
    pbuf[c, zl, x] = jnp.where(
        c == 0, pt_ref[:, 0:512].astype(F32), pt_ref[:, 512:1024].astype(F32)
    ).astype(BF16)
    loads = []
    for n, (src, dst) in enumerate(((wq_hbm, wq), (idx_hbm, idx), (slab_hbm, slab))):
        load = pltpu.make_async_copy(src, dst, local_sem.at[n])
        loads.append(load)
    loads[0].start()
    loads[1].start()

    owner = owner_ref[...]
    og, od = owner >> 4, owner & 15
    code = ((od & 3) * 4 + (og >> 2)) * 16 + (((og >> 1) & 1) * 4 + (od >> 2)) * 2 + (og & 1)
    sub, ln = iota((8, 128), 0), iota((8, 128), 1)
    count = jnp.zeros((8, 128), jnp.int32)
    for i in range(8):
        count = jnp.where(sub == i, count_ref[i], count)
    code = jnp.where(ln < count, code, -1).astype(F32)
    row = row_ref[...].astype(F32)
    high = jnp.floor(row * (1.0 / 16.0))
    low = row - 16.0 * high
    line = iota((128, 128), 0)
    kind, place = line % 16, line // 16
    upper = (line < iota((128, 128), 1)).astype(F32).astype(BF16)
    owner_line = iota((256, 128), 0).astype(F32)
    hits = [(code[i:i + 1] == owner_line).astype(F32) for i in range(8)]
    before = [jnp.dot(t.astype(BF16), upper, preferred_element_type=F32) for t in hits]
    totals = [jnp.sum(t, axis=1, keepdims=True) for t in hits]
    carry = jnp.zeros((256, 1), F32)
    table = jnp.zeros((256, 128), F32)
    for i in range(8):
        rank = jnp.sum(hits[i] * (before[i] + carry), axis=0, keepdims=True)
        carry = carry + totals[i]
        value = jnp.where(kind == 0, high[i:i + 1], jnp.where(kind == 1, low[i:i + 1], jnp.where(kind == 2, i + 1.0, 0.0)))
        value = jnp.where(rank == place.astype(F32), value, 0.0)
        table = table + nt(hits[i].astype(BF16), value.astype(BF16))
    tab[...] = table.astype(BF16).reshape(16, 16, 128)
    pl.semaphore_wait(barrier, len(peers))

    bufs = (buf_a, buf_b)
    z_sem = []
    for buf in bufs:
        s, r = send_sem(buf.at[0, 0, 0, 0:7]), recv_sem()
        for o in range(1, NZ):
            copy(buf.at[x, c, y, z], buf.at[x, c, y, z], near(0, 0, o, 0), s, r)
        z_sem.append(r)
    s, px_sem = send_sem(pbuf.at[0, 0, 0:3]), recv_sem()
    for o in range(1, NX):
        copy(pbuf.at[c, zl, x], pbuf.at[c, zl, x], near(o, 0, 0, 0), s, px_sem)

    spot = x * 4 + y
    s, ty_sem = send_sem(tab_y.at[0:15]), recv_sem()
    for i in range(NX):
        for j in range(NY):
            if i or j:
                to = near(i, j, 0, 0)
                copy(tab.at[to[0] * 4 + to[1]], tab_y.at[spot], to, s, ty_sem)
    tab_y[spot] = tab[spot]

    loads[2].start()

    loads[0].wait()
    q_own = jnp.dot(h_ref[...], wq[...], preferred_element_type=F32)
    rq_own = lax.rsqrt(jnp.mean(q_own * q_own, axis=1, keepdims=True) + EPS)
    u_own = q_own * rq_own
    pos = pos_ref[...].astype(F32)
    pos = pos * lax.rsqrt(jnp.mean(pos * pos, axis=1, keepdims=True) + EPS)
    pos_dot = jnp.sum(u_own * pos, axis=1, keepdims=True)
    pos_score = pos_dot * SCALE
    pos_exp = jnp.exp(pos_score)
    pos_dir = (pos - u_own * (pos_dot * (1.0 / E))) * (rq_own * SCALE)

    def along_x(o):
        return (o, 0, 0, 0)

    def along_y(o):
        return (0, o, 0, 0)

    mid_axis, last_axis = (along_y, along_x), (along_x, along_y)
    mid_sem, near_sem, far_sem, core_sem = [], [], [], []
    s_mid, s_near, s_far, s_core = [], [], [], []
    for buf in bufs:
        mid_sem.append([recv_sem() for _ in range(3)])
        near_sem.append([recv_sem() for _ in range(4)])
        far_sem.append(recv_sem())
        core_sem.append(recv_sem())
        s_mid.append(send_sem(buf.at[0, 0, 0:3]))
        s_near.append(send_sem(buf.at[:, 0, 0:2]))
        s_far.append(send_sem(buf.at[:, 0, 0]))
        s_core.append(send_sem(buf.at[:, 0]))

    def group(n, j, q):
        if n == 0:
            return buf_a.at[lax.rem(x - q + NX, NX), c, lax.rem(y - j + NY, NY)]
        return buf_b.at[lax.rem(x - j + NX, NX), c, lax.rem(y - q + NY, NY)]

    def to_core(n, ref):
        copy(ref, ref, near(0, 0, 0, 1), s_core[n], core_sem[n])

    def to_near(n, j):
        ref = group(n, j, 0)
        for o in (1, 3):
            copy(ref, ref, near(*last_axis[n](o)), s_near[n], near_sem[n][j])
        to_core(n, ref)

    def forward(n, j):
        await_bytes(near_sem[n][j], bufs[n].at[0, 0, 0:2])
        ahead, behind = group(n, j, 1), group(n, j, 3)
        lo, hi = ahead.at[0:4], behind.at[4:8]
        copy(lo, lo, near(*last_axis[n](1)), s_far[n], far_sem[n])
        copy(hi, hi, near(*last_axis[n](3)), s_far[n], far_sem[n])
        to_core(n, ahead)
        to_core(n, behind)

    for n, buf in enumerate(bufs):
        await_bytes(z_sem[n], buf.at[0, 0, 0, 0:7])
        ref = group(n, 0, 0)
        for o in range(1, 4):
            copy(ref, ref, near(*mid_axis[n](o)), s_mid[n], mid_sem[n][o - 1])
        to_near(n, 0)

    await_bytes(ty_sem, tab_y.at[0:15])
    tab_j[...] = jnp.swapaxes(tab_y[...].astype(F32), 0, 1).astype(BF16)
    s, tj_sem = send_sem(tab_r.at[0:15]), recv_sem()
    for o in range(NZ):
        for k in range(2):
            if o or k:
                to = near(0, 0, o, k)
                copy(tab_j.at[to[2] * 2 + to[3]], tab_r.at[z * 2 + c], to, s, tj_sem)
    tab_r[z * 2 + c] = tab_j[z * 2 + c]

    await_bytes(px_sem, pbuf.at[0, 0, 0:3])
    s, pz_sem = send_sem(pbuf.at[0, 0:3]), recv_sem()
    for o in (1, 7):
        copy(pbuf.at[c, zl], pbuf.at[c, zl], near(0, 0, o, 0), s, pz_sem)
    copy(pbuf.at[c, zl, 0:2], pbuf.at[c, zl, 0:2], near(0, 0, 2, 0), s, pz_sem)
    copy(pbuf.at[c, zl, 2:4], pbuf.at[c, zl, 2:4], near(0, 0, 6, 0), s, pz_sem)

    def middle(o):
        for n in range(2):
            await_bytes(mid_sem[n][o - 1], bufs[n].at[0, 0, 0])
            to_near(n, o)

    middle(1)
    middle(3)

    loads[1].wait()
    await_bytes(tj_sem, tab_r.at[0:15])
    src, out = iota((128, 2048), 0), iota((128, 2048), 1)
    slot, want_q = out // 256, (out // 128) % 2
    weight = jnp.where(src % 16 == 0, 16.0, 1.0)
    kept = jnp.where(want_q == 0, jnp.where(src % 16 < 2, weight, 0.0), jnp.where(src % 16 == 2, 1.0, 0.0))
    expand = jnp.where(src // 16 == slot, kept, 0.0).astype(BF16)

    def columns_of(b):
        wide = jnp.dot(tab_r[2 * b:2 * b + 2].reshape(32, 128), expand, preferred_element_type=F32)
        row = jnp.concatenate([wide[:, k * 256:k * 256 + 128] for k in range(8)], axis=0)
        qry = jnp.concatenate([wide[:, k * 256 + 128:k * 256 + 256] for k in range(8)], axis=0)
        return row, qry

    lane_f = iota((256, 128), 1).astype(F32)

    def pick(b):
        row, qry = columns_of(b)
        hot = jnp.concatenate(
            [(row == lane_f + 128.0 * t).astype(F32).astype(BF16) for t in range(16)], axis=1
        )
        r = jnp.dot(hot, idx[...], preferred_element_type=F32)
        rows[b] = r.astype(BF16)
        rr = lax.rsqrt(jnp.mean(r * r, axis=1, keepdims=True) + EPS)
        norm[b, 0] = jnp.broadcast_to(rr, (256, 128))
        norm[b, 1] = qry

    def onward(j):
        for n in range(2):
            forward(n, j)

    pick(0)
    middle(2)
    pick(1)
    onward(0)
    pick(2)
    onward(1)
    pick(3)
    pick(4)
    onward(3)
    await_bytes(pz_sem, pbuf.at[0, 0:3])
    s, pc_sem = send_sem(pbuf.at[0]), recv_sem()
    copy(pbuf.at[c], pbuf.at[c], near(0, 0, 0, 1), s, pc_sem)
    pick(5)
    onward(2)
    pick(6)
    pick(7)
    for n, buf in enumerate(bufs):
        await_bytes(far_sem[n], buf.at[:, 0, 0])
        for j in range(4):
            to_core(n, group(n, j, 2))
    for n, buf in enumerate(bufs):
        await_bytes(core_sem[n], buf.at[:, 0])

    def project(b, _):
        sides = []
        for buf in bufs:
            part = jnp.swapaxes(buf[:, :, :, b], 0, 1).astype(F32).reshape(32, 16, 256)
            sides += [part[:, 0:8].reshape(256, 256), part[:, 8:16].reshape(256, 256)]
        sides = [t.astype(BF16) for t in sides]
        for n, t in enumerate(sides):
            h_t[pl.ds(n * 256, 256), pl.ds(pl.multiple_of(b * 256, 256), 256)] = t.T
        q = jnp.dot(jnp.concatenate(sides, axis=1), wq[...], preferred_element_type=F32)
        rq = lax.rsqrt(jnp.mean(q * q, axis=1, keepdims=True) + EPS)
        u = q * rq
        hi = u.astype(BF16)
        u_two[b, 0:256] = hi
        u_two[b, 256:512] = (u - hi.astype(F32)).astype(BF16)
        u_scale[b] = jnp.broadcast_to(rq * SCALE, (256, 128))
        return 0

    lax.fori_loop(0, 8, project, 0, unroll=4)

    group_of = (iota((256, 256), 0) % 32 * 8 - 1).astype(F32)
    query_lane = iota((256, 256), 1).astype(F32)

    def score(b, _):
        r = rows[b]
        two = u_two[b]
        rr = norm[b, 0][:, 0:1]
        s = nt(two, r)
        s = (s[0:256] + s[256:512]).T * (rr * SCALE)
        qry = jnp.concatenate([norm[b, 1], norm[b, 1]], axis=1)
        live = (qry > 0.5) & (group_of + qry == query_lane)
        e = jnp.where(live, jnp.exp(s), 0.0)
        zr = jnp.sum(e, axis=0, keepdims=True)
        zbuf[b // 4, pl.ds(lax.rem(b, 4) * 2, 1), :] = zr[:, 0:128]
        zbuf[b // 4, pl.ds(lax.rem(b, 4) * 2 + 1, 1), :] = zr[:, 128:256]
        gb = tn((e * rr).astype(BF16), r)
        u = two[0:256].astype(F32) + two[256:512].astype(F32)
        gb = gb - u * (jnp.sum(u * gb, axis=1, keepdims=True) * (1.0 / E))
        ghat[pl.ds(pl.multiple_of(b * 256, 256), 256), :] = gb * u_scale[b][:, 0:1]
        return 0

    own_at = ((z * 2 + c) * 16 + x * 4 + y) * 8
    mine = jnp.sum(jnp.where(ln == lax.rem(own_at, 128) + sub, pos_exp, 0.0), axis=0, keepdims=True)
    z_sems = []

    def sums_core(k):
        zbuf[k] = zbuf[k] + jnp.where(sub + 8 * k == own_at // 128, mine, 0.0)
        s, r = send_sem(zrecv.at[k, 0]), recv_sem()
        copy(zbuf.at[k], zrecv.at[k, 0], near(0, 0, 0, 1), s, r)
        z_sems.append(r)

    def sums_xy(k):
        await_bytes(z_sems[k], zrecv.at[k, 0])
        zsum[k, 0] = zbuf[k] + zrecv[k, 0]
        s, r = send_sem(zrecv.at[k, 1:16]), recv_sem()
        n = 1
        for i in range(NX):
            for j in range(NY):
                if i or j:
                    copy(zsum.at[k, 0], zrecv.at[k, n], near(i, j, 0, 0), s, r)
                    n += 1
        return r

    def sums_z(k, r):
        await_bytes(r, zrecv.at[k, 1:16])
        total = zsum[k, 0]
        for n in range(1, 16):
            total = total + zrecv[k, n]
        zsum[k, 1] = total
        s, r = send_sem(zrecv.at[k, 16:23]), recv_sem()
        for o in range(1, NZ):
            copy(zsum.at[k, 1], zrecv.at[k, 15 + o], near(0, 0, o, 0), s, r)
        return r

    def sums_done(k, r):
        await_bytes(r, zrecv.at[k, 16:23])
        total = zsum[k, 1]
        for n in range(16, 23):
            total = total + zrecv[k, n]
        turned = jnp.concatenate([total, jnp.ones((120, 128), F32)], axis=0).T
        for t in range(8):
            zcol[pl.ds(k * 1024 + t * 128, 128), :] = jnp.broadcast_to(
                turned[:, t:t + 1], (128, 128)
            )

    def encode(lo, hi):
        def step(n, _):
            at = pl.ds(pl.multiple_of(n * 256, 256), 256)
            t = slab[at, :]
            q0, q1 = pbuf[0].reshape(E, 512), pbuf[1].reshape(E, 512)
            ren[at, :] = (nt(t[:, 0:512], q0) + nt(t[:, 512:1024], q1)).astype(BF16)
            return 0

        lax.fori_loop(lo, hi, step, 0)

    own = pl.ds(pl.multiple_of(own_at, 8), 8)

    def rescale(k):
        @pl.when(own_at // 1024 == k)
        def _():
            z_here = zcol[own, :][:, 0:1]
            ghat[own, :] = ghat[own, :] + pos_dir * (pos_exp - z_here)

        def step(b, _):
            at = pl.ds(pl.multiple_of(b * 128, 128), 128)
            gmat[at, :] = (ghat[at, :] / zcol[at, :][:, 0:1]).astype(BF16)
            return 0

        lax.fori_loop(k * 8, k * 8 + 8, step, 0)

    unit_x = [jnp.int32(1), 1 - c, jnp.int32(0)]
    first_at = [x * f + y * (1 - f) for f in unit_x]
    second_at = [y * f + x * (1 - f) for f in unit_x]
    quarter = [lax.rem(zl + 1 + n, 4) for n in range(4)]

    def product(n, k):
        at = pl.ds(pl.multiple_of(quarter[n] * 256, 256), 256)
        span = pl.ds(k * 1024, 1024)
        return jnp.dot(h_t[at, span], gmat[span, :], preferred_element_type=F32)

    def keep(n, val, more):
        for t in range(6):
            tile = val[:, t * 128:(t + 1) * 128].reshape(4, 4, 16, 128)
            if X_FIRST[t]:
                tt[n, t] = tt[n, t] + tile if more else tile
            else:
                for a in range(4):
                    for b in range(4):
                        part = tile[b, a]
                        tt[n, t, a, b] = tt[n, t, a, b] + part if more else part

    lax.fori_loop(0, 4, score, 0, unroll=4)
    sums_core(0)
    lax.fori_loop(4, 6, score, 0, unroll=2)
    xy_0 = sums_xy(0)
    lax.fori_loop(6, 8, score, 0, unroll=2)
    sums_core(1)
    za_0 = sums_z(0, xy_0)
    loads[2].wait()
    await_bytes(pc_sem, pbuf.at[0])
    encode(0, 2)
    xy_1 = sums_xy(1)
    encode(2, 5)
    sums_done(0, za_0)
    rescale(0)
    keep(0, product(0, 0), False)
    za_1 = sums_z(1, xy_1)
    for n in range(1, 4):
        keep(n, product(n, 0), False)
    encode(5, 8)
    out_copy = pltpu.make_async_copy(ren, ren_hbm, local_sem.at[3])
    out_copy.start()
    sums_done(1, za_1)
    rescale(1)

    z_own = zcol[own, :][:, 0:1]
    loss = jnp.log(z_own) - pos_score
    loss_ref[...] = jnp.sum(jnp.where(sub == ln, loss, 0.0), axis=0, keepdims=True)[:, 0:8]
    own_rows = ghat[own, :] / z_own
    own_low = own_rows - own_rows.astype(BF16).astype(F32)
    own_low = jnp.concatenate([own_low, jnp.zeros_like(own_low)], axis=0).astype(BF16)
    h_pad = jnp.concatenate([h32, jnp.zeros_like(h32)], axis=0)
    h_pad = jnp.concatenate(
        [h_pad[:, n * 256:(n + 1) * 256] for n in range(4)], axis=0
    ).astype(BF16)

    s_tc, tc_sem = send_sem(tcore), [recv_sem() for _ in range(4)]
    s_r1, r1_sem = send_sem(r1), [recv_sem() for _ in range(4)]
    s_r2, r2_sem = send_sem(r2), [recv_sem() for _ in range(4)]
    s_r3, r3_sem = send_sem(r3), recv_sem()
    hpt = h_pad.reshape(4, 16, 256)

    def produce(n):
        val = product(n, 1)
        mine = jnp.zeros((16, 256), F32)
        for t in range(4):
            mine = jnp.where(quarter[n] == t, hpt[t].astype(F32), mine)
        val = val + tn(mine.astype(BF16), own_low)
        keep(n, val, True)
        copy(tt.at[n, pl.ds((1 - c) * 3, 3)], tcore.at[n], near(0, 0, 0, 1), s_tc, tc_sem[n])

    def step_first(n):
        await_bytes(tc_sem[n], tcore.at[n])
        for u in range(3):
            f = unit_x[u]
            tsum[n, u] = tt[n, c * 3 + u] + tcore[n, u]
            for o in range(1, 4):
                to = lax.rem(first_at[u] + o, 4)
                copy(
                    tsum.at[n, u, to], r1.at[n, u, o - 1], near(o * f, o * (1 - f), 0, 0),
                    s_r1, r1_sem[n],
                )

    def step_second(n):
        await_bytes(r1_sem[n], r1.at[n])
        for u in range(3):
            f = unit_x[u]
            p1[n, u] = tsum[n, u, first_at[u]] + (r1[n, u, 0] + r1[n, u, 1] + r1[n, u, 2])
            for o in range(1, 4):
                to = lax.rem(second_at[u] + o, 4)
                copy(
                    p1.at[n, u, to], r2.at[n, u, o - 1], near(o * (1 - f), o * f, 0, 0),
                    s_r2, r2_sem[n],
                )

    def step_z(n):
        await_bytes(r2_sem[n], r2.at[n])
        for u in range(3):
            p2[n, u] = p1[n, u, second_at[u]] + (r2[n, u, 0] + r2[n, u, 1] + r2[n, u, 2])
        for k in range(2):
            if n < 3 or k:
                to = lax.rem(zl + n + 1, 4) + 4 * k
                if n == 3:
                    to = lax.rem(z + 4, 8)
                away = lax.rem(to - z + NZ, NZ)
                copy(p2.at[n], r3.at[away - 1], (x, y, to, c), s_r3, r3_sem)

    produce(0)
    produce(1)
    step_first(0)
    produce(2)
    step_first(1)
    produce(3)
    step_first(2)
    step_second(0)
    step_first(3)
    step_second(1)
    step_z(0)
    step_second(2)
    step_z(1)
    step_second(3)
    step_z(2)
    step_z(3)
    await_bytes(r3_sem, r3)
    done = p2[3]
    for o in range(NZ - 1):
        done = done + r3[o]
    at = y * 2 + c
    fin[at] = done
    s, r = send_sem(fin.at[0:7]), recv_sem()
    for o in range(NY):
        for k in range(2):
            if o or k:
                copy(fin.at[at], fin.at[at], near(0, o, 0, k), s, r)
    await_bytes(r, fin.at[0:7])
    for j in range(NY):
        for n in range(2):
            for u in range(3):
                grad_ref[pl.ds(j * 16, 16), pl.ds(n * 384 + u * 128, 128)] = fin[j * 2 + n, u]
    for sem, ref in sends:
        await_bytes(sem, ref)
    out_copy.wait()
    assert (used_s[0], used_r[0]) == (SENDS, RECVS)


def hand_over(loss_in, grad_in, ren_in, loss_out, grad_out, ren_out, held, sem):
    parts = 4
    size = ren_in.shape[0] // parts
    ins, outs = [], []
    for n in range(parts):
        at = pl.ds(n * size, size)
        ins.append(pltpu.make_async_copy(ren_in.at[at], held.at[at], sem.at[n]))
        outs.append(pltpu.make_async_copy(held.at[at], ren_out.at[at], sem.at[parts + n]))
    for copy in ins:
        copy.start()
    loss_out[...] = loss_in[...]
    grad_out[...] = grad_in[...]
    for first, then in zip(ins, outs):
        first.wait()
        then.start()
    for copy in outs:
        copy.wait()


SENDS = 26
RECVS = 45


def local(
    question_encoder_states,
    query_proj,
    positive_embed,
    stale_index,
    neg_owner,
    neg_row,
    neg_count,
    slab_hidden,
    passage_projector,
):
    vmem = pl.BlockSpec(memory_space=pltpu.VMEM)
    smem = pl.BlockSpec(memory_space=pltpu.SMEM)
    hbm = pl.BlockSpec(memory_space=pl.ANY)
    V = pltpu.VMEM
    scratch = [
        V((D, E), BF16), V((2048, E), BF16), V((2048, D), BF16), V((2048, E), BF16),
        pltpu.SemaphoreType.DMA((4,)),
        V((NX, 2, NY, NZ, 16, 256), BF16), V((NX, 2, NY, NZ, 16, 256), BF16),
        V((D, 2048), BF16),
        V((16, 16, 128), BF16), V((16, 16, 128), BF16), V((16, 16, 128), BF16),
        V((16, 16, 128), BF16),
        V((2, 4, 4, 48, 512), BF16), V((8, 256, E), BF16), V((8, 2, 256, 128), F32),
        V((8, 512, E), BF16), V((8, 256, 128), F32),
        V((2048, E), F32), V((2048, E), BF16),
        V((2, 8, 128), F32), V((2, 23, 8, 128), F32), V((2, 2, 8, 128), F32), V((2048, 128), F32),
        V((4, 6, 4, 4, 16, 128), F32), V((4, 3, 4, 4, 16, 128), F32),
        V((4, 3, 4, 4, 16, 128), F32),
        V((4, 3, 3, 4, 16, 128), F32), V((4, 3, 4, 16, 128), F32),
        V((4, 3, 3, 16, 128), F32), V((4, 3, 16, 128), F32),
        V((NZ - 1, 3, 16, 128), F32), V((NY * 2, 3, 16, 128), F32),
        pltpu.SemaphoreType.DMA((SENDS,)), pltpu.SemaphoreType.DMA((RECVS,)),
    ]
    shapes = (
        jax.ShapeDtypeStruct((1, 8), F32),
        jax.ShapeDtypeStruct((64, E), F32),
        jax.ShapeDtypeStruct((2048, E), BF16),
    )
    results = pl.pallas_call(
        body,
        out_shape=shapes,
        in_specs=[vmem, vmem, vmem, smem, vmem, vmem, hbm, hbm, hbm],
        out_specs=(vmem, vmem, hbm),
        scratch_shapes=scratch,
        compiler_params=pltpu.CompilerParams(
            collective_id=0, has_side_effects=True, vmem_limit_bytes=62 * 2**20
        ),
        cost_estimate=pl.CostEstimate(
            flops=30 * 10**9, bytes_accessed=16 * 2**20, transcendentals=2**20
        ),
    )(
        question_encoder_states, neg_owner[..., 0], neg_row, neg_count, positive_embed,
        passage_projector.T, query_proj, stale_index, slab_hidden,
    )
    losses, grad, renewed = pl.pallas_call(
        hand_over,
        out_shape=shapes,
        in_specs=[vmem, vmem, hbm],
        out_specs=(vmem, vmem, hbm),
        scratch_shapes=[V((2048, E), BF16), pltpu.SemaphoreType.DMA((8,))],
        compiler_params=pltpu.CompilerParams(vmem_limit_bytes=62 * 2**20),
    )(*results)
    return losses.reshape(8), grad, renewed


def solution(mesh):
    rows = P(("group", "dev"), None)
    in_specs = (
        rows, P(), rows, rows, P(("group", "dev"), None, None), rows,
        P(("group", "dev")), rows, P(None, "dev"),
    )
    out_specs = (P(("group", "dev")), P("dev", None), rows)
    return jax.shard_map(local, mesh=mesh, in_specs=in_specs, out_specs=out_specs, check_vma=False)
```

```python
import jax
import jax.numpy as jnp
from jax import lax
from jax.experimental import pallas as pl
from jax.experimental.pallas import tpu as pltpu
from jax.sharding import PartitionSpec as P

MESH = pl.DeviceIdType.MESH
F32 = jnp.float32
BF16 = jnp.bfloat16
EPS = 1e-06
DIV = 0.05
E = 768
D = 1024
SCALE = 1.0 / (E * DIV)
NX, NY, NZ = 4, 4, 8


def iota(shape, dim):
    return lax.broadcasted_iota(jnp.int32, shape, dim)


def nt(a, b):
    return lax.dot_general(a, b, (((1,), (1,)), ((), ())), preferred_element_type=F32)


def tn(a, b):
    return lax.dot_general(a, b, (((0,), (0,)), ((), ())), preferred_element_type=F32)


def device_of(x, y, z, c):
    return ((y * 2 + z // 4) * 2 + c, lax.rem(z, 4) * 4 + x)


def body(
    h_ref, owner_ref, row_ref, count_ref, pos_ref, pt_ref, wq_hbm, idx_hbm, slab_hbm,
    loss_ref, grad_ref, ren_hbm,
    wq, idx, slab, ren, local_sem,
    buf_a, buf_b, h_t, tab, tab_y, tab_j, tab_r,
    pbuf, rows, norm, u_two, u_scale, ghat, gother, posd, posd_in, gmat, zbuf, zrecv, zsum, zcol,
    tt, r1, p1, r2, p2, r3, fin,
    ssem, rsem,
):
    g = lax.axis_index("group")
    d = lax.axis_index("dev")
    x = lax.rem(d, 4)
    c = lax.rem(g, 2)
    y = g // 4
    zl = d // 4
    z = lax.rem(g // 2, 2) * 4 + zl

    def near(dx, dy, dz, dc):
        return (
            lax.rem(x + dx + NX, NX),
            lax.rem(y + dy + NY, NY),
            lax.rem(z + dz + NZ, NZ),
            lax.rem(c + dc, 2),
        )

    used_s, used_r, sends = [0], [0], []

    def send_sem(ref):
        n = used_s[0]
        used_s[0] = n + 1
        sends.append((ssem.at[n], ref))
        return ssem.at[n]

    def recv_sem():
        n = used_r[0]
        used_r[0] = n + 1
        return rsem.at[n]

    def await_bytes(sem, ref):
        pltpu.make_async_copy(ref, ref, sem).wait()

    def copy(src, dst, at, s_sem, r_sem):
        pltpu.make_async_remote_copy(
            src_ref=src, dst_ref=dst, send_sem=s_sem, recv_sem=r_sem,
            device_id=device_of(*at), device_id_type=MESH,
        ).start()

    peers = [(0, 0, i, 0) for i in range(1, NZ)]
    peers += [(i, j, 0, 0) for i in range(NX) for j in range(NY) if i or j]
    peers += [(0, 0, i, 1) for i in range(NZ)]
    peers += [(0, j, 0, 1) for j in range(1, NY)]
    barrier = pltpu.get_barrier_semaphore()
    for p in peers:
        pl.semaphore_signal(barrier, inc=1, device_id=device_of(*near(*p)), device_id_type=MESH)

    h32 = h_ref[...].astype(F32)
    buf_a[x, c, y, z] = jnp.concatenate([h32[:, 0:256], h32[:, 256:512]], axis=0).astype(BF16)
    buf_b[x, c, y, z] = jnp.concatenate([h32[:, 512:768], h32[:, 768:1024]], axis=0).astype(BF16)
    pbuf[c, zl, x] = jnp.where(
        c == 0, pt_ref[:, 0:512].astype(F32), pt_ref[:, 512:1024].astype(F32)
    ).astype(BF16)
    loads = []
    for n, (src, dst) in enumerate(((wq_hbm, wq), (idx_hbm, idx), (slab_hbm, slab))):
        load = pltpu.make_async_copy(src, dst, local_sem.at[n])
        loads.append(load)
    loads[0].start()
    loads[1].start()

    owner = owner_ref[...]
    og, od = owner >> 4, owner & 15
    code = ((od & 3) * 4 + (og >> 2)) * 16 + (((og >> 1) & 1) * 4 + (od >> 2)) * 2 + (og & 1)
    sub, ln = iota((8, 128), 0), iota((8, 128), 1)
    count = jnp.zeros((8, 128), jnp.int32)
    for i in range(8):
        count = jnp.where(sub == i, count_ref[i], count)
    code = jnp.where(ln < count, code, -1).astype(F32)
    row = row_ref[...].astype(F32)
    high = jnp.floor(row * (1.0 / 16.0))
    low = row - 16.0 * high
    line = iota((128, 128), 0)
    kind, place = line % 16, line // 16
    upper = (line < iota((128, 128), 1)).astype(F32).astype(BF16)
    owner_line = iota((256, 128), 0).astype(F32)
    hits = [(code[i:i + 1] == owner_line).astype(F32) for i in range(8)]
    before = [jnp.dot(t.astype(BF16), upper, preferred_element_type=F32) for t in hits]
    totals = [jnp.sum(t, axis=1, keepdims=True) for t in hits]
    carry = jnp.zeros((256, 1), F32)
    table = jnp.zeros((256, 128), F32)
    for i in range(8):
        rank = jnp.sum(hits[i] * (before[i] + carry), axis=0, keepdims=True)
        carry = carry + totals[i]
        value = jnp.where(kind == 0, high[i:i + 1], jnp.where(kind == 1, low[i:i + 1], jnp.where(kind == 2, i + 1.0, 0.0)))
        value = jnp.where(rank == place.astype(F32), value, 0.0)
        table = table + nt(hits[i].astype(BF16), value.astype(BF16))
    tab[...] = table.astype(BF16).reshape(16, 16, 128)
    pl.semaphore_wait(barrier, len(peers))

    bufs = (buf_a, buf_b)
    z_sem = []
    for buf in bufs:
        s, r = send_sem(buf.at[0, 0, 0, 0:7]), recv_sem()
        for o in range(1, NZ):
            copy(buf.at[x, c, y, z], buf.at[x, c, y, z], near(0, 0, o, 0), s, r)
        z_sem.append(r)
    s, px_sem = send_sem(pbuf.at[0, 0, 0:3]), recv_sem()
    for o in range(1, NX):
        copy(pbuf.at[c, zl, x], pbuf.at[c, zl, x], near(o, 0, 0, 0), s, px_sem)

    spot = x * 4 + y
    s, ty_sem = send_sem(tab_y.at[0:15]), recv_sem()
    for i in range(NX):
        for j in range(NY):
            if i or j:
                to = near(i, j, 0, 0)
                copy(tab.at[to[0] * 4 + to[1]], tab_y.at[spot], to, s, ty_sem)
    tab_y[spot] = tab[spot]

    loads[2].start()

    await_bytes(ty_sem, tab_y.at[0:15])
    tab_j[...] = jnp.swapaxes(tab_y[...].astype(F32), 0, 1).astype(BF16)
    s, tj_sem = send_sem(tab_r.at[0:15]), recv_sem()
    for o in range(NZ):
        for k in range(2):
            if o or k:
                to = near(0, 0, o, k)
                copy(tab_j.at[to[2] * 2 + to[3]], tab_r.at[z * 2 + c], to, s, tj_sem)
    tab_r[z * 2 + c] = tab_j[z * 2 + c]

    loads[0].wait()
    q_own = jnp.dot(h_ref[...], wq[...], preferred_element_type=F32)
    rq_own = lax.rsqrt(jnp.mean(q_own * q_own, axis=1, keepdims=True) + EPS)
    u_own = q_own * rq_own
    pos = pos_ref[...].astype(F32)
    pos = pos * lax.rsqrt(jnp.mean(pos * pos, axis=1, keepdims=True) + EPS)
    pos_dot = jnp.sum(u_own * pos, axis=1, keepdims=True)
    pos_score = pos_dot * SCALE
    pos_exp = jnp.exp(pos_score)
    pos_dir = (pos - u_own * (pos_dot * (1.0 / E))) * (rq_own * SCALE)
    for k in range(2):
        posd[k] = pos_dir[:, k * 384:(k + 1) * 384]
    s, posd_sem = send_sem(posd.at[0]), recv_sem()
    copy(posd.at[1 - c], posd_in, near(0, 0, 0, 1), s, posd_sem)

    def along_x(o):
        return (o, 0, 0, 0)

    def along_y(o):
        return (0, o, 0, 0)

    mid_axis, last_axis = (along_y, along_x), (along_x, along_y)
    mid_sem, near_sem, far_sem, core_sem = [], [], [], []
    s_mid, s_near, s_far, s_core = [], [], [], []
    for buf in bufs:
        mid_sem.append([recv_sem() for _ in range(3)])
        near_sem.append([recv_sem() for _ in range(4)])
        far_sem.append(recv_sem())
        core_sem.append(recv_sem())
        s_mid.append(send_sem(buf.at[0, 0, 0:3]))
        s_near.append(send_sem(buf.at[:, 0, 0:2]))
        s_far.append(send_sem(buf.at[:, 0, 0]))
        s_core.append(send_sem(buf.at[:, 0]))

    def group(n, j, q):
        if n == 0:
            return buf_a.at[lax.rem(x - q + NX, NX), c, lax.rem(y - j + NY, NY)]
        return buf_b.at[lax.rem(x - j + NX, NX), c, lax.rem(y - q + NY, NY)]

    def to_core(n, ref):
        copy(ref, ref, near(0, 0, 0, 1), s_core[n], core_sem[n])

    def to_near(n, j):
        ref = group(n, j, 0)
        for o in (1, 3):
            copy(ref, ref, near(*last_axis[n](o)), s_near[n], near_sem[n][j])
        to_core(n, ref)

    def forward(n, j):
        await_bytes(near_sem[n][j], bufs[n].at[0, 0, 0:2])
        ahead, behind = group(n, j, 1), group(n, j, 3)
        lo, hi = ahead.at[0:4], behind.at[4:8]
        copy(lo, lo, near(*last_axis[n](1)), s_far[n], far_sem[n])
        copy(hi, hi, near(*last_axis[n](3)), s_far[n], far_sem[n])
        to_core(n, ahead)
        to_core(n, behind)

    for n, buf in enumerate(bufs):
        await_bytes(z_sem[n], buf.at[0, 0, 0, 0:7])
        ref = group(n, 0, 0)
        for o in range(1, 4):
            copy(ref, ref, near(*mid_axis[n](o)), s_mid[n], mid_sem[n][o - 1])
        to_near(n, 0)

    await_bytes(px_sem, pbuf.at[0, 0, 0:3])
    s, pz_sem = send_sem(pbuf.at[0, 0:3]), recv_sem()
    for o in (1, 7):
        copy(pbuf.at[c, zl], pbuf.at[c, zl], near(0, 0, o, 0), s, pz_sem)
    copy(pbuf.at[c, zl, 0:2], pbuf.at[c, zl, 0:2], near(0, 0, 2, 0), s, pz_sem)
    copy(pbuf.at[c, zl, 2:4], pbuf.at[c, zl, 2:4], near(0, 0, 6, 0), s, pz_sem)

    def middle(o):
        for n in range(2):
            await_bytes(mid_sem[n][o - 1], bufs[n].at[0, 0, 0])
            to_near(n, o)

    middle(1)
    middle(3)

    loads[1].wait()
    await_bytes(tj_sem, tab_r.at[0:15])
    src, out = iota((128, 2048), 0), iota((128, 2048), 1)
    slot, want_q = out // 256, (out // 128) % 2
    weight = jnp.where(src % 16 == 0, 16.0, 1.0)
    kept = jnp.where(want_q == 0, jnp.where(src % 16 < 2, weight, 0.0), jnp.where(src % 16 == 2, 1.0, 0.0))
    expand = jnp.where(src // 16 == slot, kept, 0.0).astype(BF16)

    def columns_of(b):
        wide = jnp.dot(tab_r[2 * b:2 * b + 2].reshape(32, 128), expand, preferred_element_type=F32)
        row = jnp.concatenate([wide[:, k * 256:k * 256 + 128] for k in range(8)], axis=0)
        qry = jnp.concatenate([wide[:, k * 256 + 128:k * 256 + 256] for k in range(8)], axis=0)
        return row, qry

    lane_f = iota((256, 128), 1).astype(F32)

    def pick(b):
        row, qry = columns_of(b)
        hot = jnp.concatenate(
            [(row == lane_f + 128.0 * t).astype(F32).astype(BF16) for t in range(16)], axis=1
        )
        r = jnp.dot(hot, idx[...], preferred_element_type=F32)
        rows[b] = r.astype(BF16)
        rr = lax.rsqrt(jnp.mean(r * r, axis=1, keepdims=True) + EPS)
        norm[b, 0] = jnp.broadcast_to(rr, (256, 128))
        norm[b, 1] = qry

    def onward(j):
        for n in range(2):
            forward(n, j)

    pick(0)
    middle(2)
    pick(1)
    onward(0)
    pick(2)
    onward(1)
    pick(3)
    pick(4)
    onward(3)
    await_bytes(pz_sem, pbuf.at[0, 0:3])
    s, pc_sem = send_sem(pbuf.at[0]), recv_sem()
    copy(pbuf.at[c], pbuf.at[c], near(0, 0, 0, 1), s, pc_sem)
    pick(5)
    onward(2)
    pick(6)
    pick(7)
    for n, buf in enumerate(bufs):
        await_bytes(far_sem[n], buf.at[:, 0, 0])
        for j in range(4):
            to_core(n, group(n, j, 2))
    for n, buf in enumerate(bufs):
        await_bytes(core_sem[n], buf.at[:, 0])

    def project(b, _):
        sides = []
        for buf in bufs:
            part = jnp.swapaxes(buf[:, :, :, b], 0, 1).astype(F32).reshape(32, 16, 256)
            sides += [part[:, 0:8].reshape(256, 256), part[:, 8:16].reshape(256, 256)]
        sides = [t.astype(BF16) for t in sides]
        for n, t in enumerate(sides):
            h_t[pl.ds(n * 256, 256), pl.ds(pl.multiple_of(b * 256, 256), 256)] = t.T
        q = jnp.dot(jnp.concatenate(sides, axis=1), wq[...], preferred_element_type=F32)
        rq = lax.rsqrt(jnp.mean(q * q, axis=1, keepdims=True) + EPS)
        u = q * rq
        hi = u.astype(BF16)
        u_two[b, 0:256] = hi
        u_two[b, 256:512] = (u - hi.astype(F32)).astype(BF16)
        u_scale[b] = jnp.broadcast_to(rq * SCALE, (256, 128))
        return 0

    lax.fori_loop(0, 8, project, 0, unroll=4)

    group_of = (iota((256, 256), 0) % 32 * 8 - 1).astype(F32)
    query_lane = iota((256, 256), 1).astype(F32)

    def score(b, _):
        r = rows[b]
        two = u_two[b]
        rr = norm[b, 0][:, 0:1]
        s = nt(two, r)
        s = (s[0:256] + s[256:512]).T * (rr * SCALE)
        qry = jnp.concatenate([norm[b, 1], norm[b, 1]], axis=1)
        live = (qry > 0.5) & (group_of + qry == query_lane)
        e = jnp.where(live, jnp.exp(s), 0.0)
        zr = jnp.sum(e, axis=0, keepdims=True)
        zbuf[b // 4, pl.ds(lax.rem(b, 4) * 2, 1), :] = zr[:, 0:128]
        zbuf[b // 4, pl.ds(lax.rem(b, 4) * 2 + 1, 1), :] = zr[:, 128:256]
        gb = tn((e * rr).astype(BF16), r)
        u = two[0:256].astype(F32) + two[256:512].astype(F32)
        gb = gb - u * (jnp.sum(u * gb, axis=1, keepdims=True) * (1.0 / E))
        gb = gb * u_scale[b][:, 0:1]
        at = pl.ds(pl.multiple_of(b * 256, 256), 256)
        ghat[0, at, :] = gb[:, 0:384]
        ghat[1, at, :] = gb[:, 384:768]
        return 0

    own_at = ((z * 2 + c) * 16 + x * 4 + y) * 8
    mine = jnp.sum(jnp.where(ln == lax.rem(own_at, 128) + sub, pos_exp, 0.0), axis=0, keepdims=True)
    z_sems = []

    def sums_core(k):
        zbuf[k] = zbuf[k] + jnp.where(sub + 8 * k == own_at // 128, mine, 0.0)
        s, r = send_sem(zrecv.at[k, 0]), recv_sem()
        copy(zbuf.at[k], zrecv.at[k, 0], near(0, 0, 0, 1), s, r)
        z_sems.append(r)

    def sums_xy(k):
        await_bytes(z_sems[k], zrecv.at[k, 0])
        zsum[k, 0] = zbuf[k] + zrecv[k, 0]
        s, r = send_sem(zrecv.at[k, 1:16]), recv_sem()
        n = 1
        for i in range(NX):
            for j in range(NY):
                if i or j:
                    copy(zsum.at[k, 0], zrecv.at[k, n], near(i, j, 0, 0), s, r)
                    n += 1
        return r

    def sums_z(k, r):
        await_bytes(r, zrecv.at[k, 1:16])
        total = zsum[k, 0]
        for n in range(1, 16):
            total = total + zrecv[k, n]
        zsum[k, 1] = total
        s, r = send_sem(zrecv.at[k, 16:23]), recv_sem()
        for o in range(1, NZ):
            copy(zsum.at[k, 1], zrecv.at[k, 15 + o], near(0, 0, o, 0), s, r)
        return r

    def sums_done(k, r):
        await_bytes(r, zrecv.at[k, 16:23])
        total = zsum[k, 1]
        for n in range(16, 23):
            total = total + zrecv[k, n]
        turned = jnp.concatenate([total, jnp.ones((120, 128), F32)], axis=0).T
        for t in range(8):
            zcol[pl.ds(k * 1024 + t * 128, 128), :] = jnp.broadcast_to(
                turned[:, t:t + 1], (128, 128)
            )

    def encode(lo, hi):
        def step(n, _):
            at = pl.ds(pl.multiple_of(n * 256, 256), 256)
            t = slab[at, :]
            q0, q1 = pbuf[0].reshape(E, 512), pbuf[1].reshape(E, 512)
            ren[at, :] = (nt(t[:, 0:512], q0) + nt(t[:, 512:1024], q1)).astype(BF16)
            return 0

        lax.fori_loop(lo, hi, step, 0)

    own = pl.ds(pl.multiple_of(own_at, 8), 8)
    partner = pl.ds(pl.multiple_of(((z * 2 + 1 - c) * 16 + x * 4 + y) * 8, 8), 8)
    g_sems = []

    def terms_core(k):
        @pl.when(own_at // 1024 == k)
        def _():
            for t in range(2):
                ghat[t, own, :] = ghat[t, own, :] + posd[t] * pos_exp

        span = pl.ds(k * 1024, 1024)
        s, r = send_sem(gother.at[span]), recv_sem()
        copy(ghat.at[1 - c, span], gother.at[span], near(0, 0, 0, 1), s, r)
        g_sems.append(r)

    def rescale(k):
        await_bytes(g_sems[k], gother.at[pl.ds(k * 1024, 1024)])

        @pl.when(own_at // 1024 == k)
        def _():
            ghat[c, own, :] = ghat[c, own, :] - posd[c] * zcol[own, :][:, 0:1]
            ghat[c, partner, :] = ghat[c, partner, :] - posd_in[...] * zcol[partner, :][:, 0:1]

        def step(b, _):
            at = pl.ds(pl.multiple_of(b * 128, 128), 128)
            gmat[at, :] = ((ghat[c, at, :] + gother[at, :]) / zcol[at, :][:, 0:1]).astype(BF16)
            return 0

        lax.fori_loop(k * 8, k * 8 + 8, step, 0, unroll=4)

    unit_x = [1, 1 - c, 0]
    first_at = [x * f + y * (1 - f) for f in unit_x]
    second_at = [y * f + x * (1 - f) for f in unit_x]
    quarter = [lax.rem(zl + 1 + n, 4) for n in range(4)]

    def product(n, k):
        at = pl.ds(pl.multiple_of(quarter[n] * 256, 256), 256)
        span = pl.ds(k * 1024, 1024)
        return jnp.dot(h_t[at, span], gmat[span, :], preferred_element_type=F32)

    def keep(n, val, more):
        for u in range(3):
            tile = val[:, u * 128:(u + 1) * 128].reshape(4, 4, 16, 128)
            if u == 0:
                tt[n, u] = tt[n, u] + tile if more else tile
                continue
            for i in range(4):
                for j in range(4):
                    a = i * unit_x[u] + j * (1 - unit_x[u])
                    b = j * unit_x[u] + i * (1 - unit_x[u])
                    part = tile[i, j]
                    tt[n, u, a, b] = tt[n, u, a, b] + part if more else part

    lax.fori_loop(0, 4, score, 0, unroll=4)
    sums_core(0)
    terms_core(0)
    lax.fori_loop(4, 6, score, 0, unroll=2)
    xy_0 = sums_xy(0)
    lax.fori_loop(6, 8, score, 0, unroll=2)
    sums_core(1)
    terms_core(1)
    za_0 = sums_z(0, xy_0)
    loads[2].wait()
    await_bytes(pc_sem, pbuf.at[0])
    encode(0, 1)
    xy_1 = sums_xy(1)
    encode(1, 3)
    sums_done(0, za_0)
    await_bytes(posd_sem, posd_in)
    rescale(0)
    za_1 = sums_z(1, xy_1)
    for n in range(4):
        keep(n, product(n, 0), False)
    encode(3, 4)
    sums_done(1, za_1)
    rescale(1)

    z_own = zcol[own, :][:, 0:1]
    loss = jnp.log(z_own) - pos_score
    loss_ref[...] = jnp.sum(jnp.where(sub == ln, loss, 0.0), axis=0, keepdims=True)[:, 0:8]
    pair_rows = jnp.concatenate(
        [(ghat[c, at, :] + gother[at, :]) / zcol[at, :][:, 0:1] for at in (own, partner)], axis=0
    )
    pair_low = (pair_rows - pair_rows.astype(BF16).astype(F32)).astype(BF16)
    pair_h = []
    for buf in bufs:
        mine, its = buf[x, c, y, z].astype(F32), buf[x, 1 - c, y, z].astype(F32)
        for at in (slice(0, 8), slice(8, 16)):
            pair_h.append(jnp.concatenate([mine[at], its[at]], axis=0))

    s_r1, r1_sem = send_sem(r1), [recv_sem() for _ in range(4)]
    s_r2, r2_sem = send_sem(r2), [recv_sem() for _ in range(4)]
    s_r3, r3_sem = send_sem(r3), recv_sem()

    def produce(n):
        val = product(n, 1)
        mine = jnp.zeros((16, 256), F32)
        for t in range(4):
            mine = jnp.where(quarter[n] == t, pair_h[t], mine)
        val = val + tn(mine.astype(BF16), pair_low)
        keep(n, val, True)

    def step_first(n):
        for u in range(3):
            f = unit_x[u]
            for o in range(1, 4):
                to = lax.rem(first_at[u] + o, 4)
                copy(
                    tt.at[n, u, to], r1.at[n, u, o - 1], near(o * f, o * (1 - f), 0, 0),
                    s_r1, r1_sem[n],
                )

    def step_second(n):
        await_bytes(r1_sem[n], r1.at[n])
        for u in range(3):
            f = unit_x[u]
            p1[n, u] = tt[n, u, first_at[u]] + (r1[n, u, 0] + r1[n, u, 1] + r1[n, u, 2])
            for o in range(1, 4):
                to = lax.rem(second_at[u] + o, 4)
                copy(
                    p1.at[n, u, to], r2.at[n, u, o - 1], near(o * (1 - f), o * f, 0, 0),
                    s_r2, r2_sem[n],
                )

    def step_z(n):
        await_bytes(r2_sem[n], r2.at[n])
        for u in range(3):
            p2[n, u] = p1[n, u, second_at[u]] + (r2[n, u, 0] + r2[n, u, 1] + r2[n, u, 2])
        for k in range(2):
            if n < 3 or k:
                to = lax.rem(zl + n + 1, 4) + 4 * k
                if n == 3:
                    to = lax.rem(z + 4, 8)
                away = lax.rem(to - z + NZ, NZ)
                copy(p2.at[n], r3.at[away - 1], (x, y, to, c), s_r3, r3_sem)

    for n in range(4):
        produce(n)
        step_first(n)
    encode(4, 5)
    step_second(0)
    encode(5, 6)
    step_second(1)
    step_z(0)
    encode(6, 7)
    step_second(2)
    step_z(1)
    encode(7, 8)
    out_copy = pltpu.make_async_copy(ren, ren_hbm, local_sem.at[3])
    out_copy.start()
    step_second(3)
    step_z(2)
    step_z(3)
    await_bytes(r3_sem, r3)
    done = p2[3]
    for o in range(NZ - 1):
        done = done + r3[o]
    at = y * 2 + c
    fin[at] = done
    s, r = send_sem(fin.at[0:7]), recv_sem()
    for o in range(NY):
        for k in range(2):
            if o or k:
                copy(fin.at[at], fin.at[at], near(0, o, 0, k), s, r)
    await_bytes(r, fin.at[0:7])
    for j in range(NY):
        for n in range(2):
            for u in range(3):
                grad_ref[pl.ds(j * 16, 16), pl.ds(n * 384 + u * 128, 128)] = fin[j * 2 + n, u]
    for sem, ref in sends:
        await_bytes(sem, ref)
    out_copy.wait()
    assert (used_s[0], used_r[0]) == (SENDS, RECVS)


def hand_over(loss_in, grad_in, ren_in, loss_out, grad_out, ren_out, held, sem):
    parts = 2
    size = ren_in.shape[0] // parts
    ins, outs = [], []
    for n in range(parts):
        at = pl.ds(n * size, size)
        ins.append(pltpu.make_async_copy(ren_in.at[at], held.at[at], sem.at[n]))
        outs.append(pltpu.make_async_copy(held.at[at], ren_out.at[at], sem.at[parts + n]))
    for copy in ins:
        copy.start()
    loss_out[...] = loss_in[...]
    grad_out[...] = grad_in[...]
    for first, then in zip(ins, outs):
        first.wait()
        then.start()
    for copy in outs:
        copy.wait()


SENDS = 28
RECVS = 44


def local(
    question_encoder_states,
    query_proj,
    positive_embed,
    stale_index,
    neg_owner,
    neg_row,
    neg_count,
    slab_hidden,
    passage_projector,
):
    vmem = pl.BlockSpec(memory_space=pltpu.VMEM)
    smem = pl.BlockSpec(memory_space=pltpu.SMEM)
    hbm = pl.BlockSpec(memory_space=pl.ANY)
    V = pltpu.VMEM
    scratch = [
        V((D, E), BF16), V((2048, E), BF16), V((2048, D), BF16), V((2048, E), BF16),
        pltpu.SemaphoreType.DMA((4,)),
        V((NX, 2, NY, NZ, 16, 256), BF16), V((NX, 2, NY, NZ, 16, 256), BF16),
        V((D, 2048), BF16),
        V((16, 16, 128), BF16), V((16, 16, 128), BF16), V((16, 16, 128), BF16),
        V((16, 16, 128), BF16),
        V((2, 4, 4, 48, 512), BF16), V((8, 256, E), BF16), V((8, 2, 256, 128), F32),
        V((8, 512, E), BF16), V((8, 256, 128), F32),
        V((2, 2048, 384), F32), V((2048, 384), F32), V((2, 8, 384), F32), V((8, 384), F32),
        V((2048, 384), BF16),
        V((2, 8, 128), F32), V((2, 23, 8, 128), F32), V((2, 2, 8, 128), F32), V((2048, 128), F32),
        V((4, 3, 4, 4, 16, 128), F32),
        V((4, 3, 3, 4, 16, 128), F32), V((4, 3, 4, 16, 128), F32),
        V((4, 3, 3, 16, 128), F32), V((4, 3, 16, 128), F32),
        V((NZ - 1, 3, 16, 128), F32), V((NY * 2, 3, 16, 128), F32),
        pltpu.SemaphoreType.DMA((SENDS,)), pltpu.SemaphoreType.DMA((RECVS,)),
    ]
    shapes = (
        jax.ShapeDtypeStruct((1, 8), F32),
        jax.ShapeDtypeStruct((64, E), F32),
        jax.ShapeDtypeStruct((2048, E), BF16),
    )
    results = pl.pallas_call(
        body,
        out_shape=shapes,
        in_specs=[vmem, vmem, vmem, smem, vmem, vmem, hbm, hbm, hbm],
        out_specs=(vmem, vmem, hbm),
        scratch_shapes=scratch,
        compiler_params=pltpu.CompilerParams(
            collective_id=0, has_side_effects=True, vmem_limit_bytes=62 * 2**20
        ),
        cost_estimate=pl.CostEstimate(
            flops=30 * 10**9, bytes_accessed=16 * 2**20, transcendentals=2**20
        ),
    )(
        question_encoder_states, neg_owner[..., 0], neg_row, neg_count, positive_embed,
        passage_projector.T, query_proj, stale_index, slab_hidden,
    )
    losses, grad, renewed = pl.pallas_call(
        hand_over,
        out_shape=shapes,
        in_specs=[vmem, vmem, hbm],
        out_specs=(vmem, vmem, hbm),
        scratch_shapes=[V((2048, E), BF16), pltpu.SemaphoreType.DMA((4,))],
        compiler_params=pltpu.CompilerParams(vmem_limit_bytes=62 * 2**20),
    )(*results)
    return losses.reshape(8), grad, renewed


def solution(mesh):
    rows = P(("group", "dev"), None)
    in_specs = (
        rows, P(), rows, rows, P(("group", "dev"), None, None), rows,
        P(("group", "dev")), rows, P(None, "dev"),
    )
    out_specs = (P(("group", "dev")), P("dev", None), rows)
    return jax.shard_map(local, mesh=mesh, in_specs=in_specs, out_specs=out_specs, check_vma=False)
```

```python
import jax
import jax.numpy as jnp
from jax import lax
from jax.experimental import pallas as pl
from jax.experimental.pallas import tpu as pltpu
from jax.sharding import PartitionSpec as P

MESH = pl.DeviceIdType.MESH
F32 = jnp.float32
BF16 = jnp.bfloat16
EPS = 1e-06
DIV = 0.05
E = 768
D = 1024
SCALE = 1.0 / (E * DIV)
NX, NY, NZ = 4, 4, 8


def iota(shape, dim):
    return lax.broadcasted_iota(jnp.int32, shape, dim)


def nt(a, b):
    return lax.dot_general(a, b, (((1,), (1,)), ((), ())), preferred_element_type=F32)


def tn(a, b):
    return lax.dot_general(a, b, (((0,), (0,)), ((), ())), preferred_element_type=F32)


def device_of(x, y, z, c):
    return ((y * 2 + z // 4) * 2 + c, lax.rem(z, 4) * 4 + x)


def body(
    h_ref, owner_ref, row_ref, count_ref, pos_ref, pt_ref, wq_hbm, idx_hbm, slab_hbm,
    loss_ref, grad_ref, ren_hbm,
    wq, idx, slab, ren, local_sem,
    buf_a, buf_b, h_t, tab, tab_y, tab_j, tab_r,
    pbuf, rows, norm, u_two, u_scale, ghat, gother, posd, posd_in, gmat, zbuf, zrecv, zsum, zcol,
    tt, r1, p1, r2, p2, r3, fin,
    ssem, rsem,
):
    g = lax.axis_index("group")
    d = lax.axis_index("dev")
    x = lax.rem(d, 4)
    c = lax.rem(g, 2)
    y = g // 4
    zl = d // 4
    z = lax.rem(g // 2, 2) * 4 + zl

    def near(dx, dy, dz, dc):
        return (
            lax.rem(x + dx + NX, NX),
            lax.rem(y + dy + NY, NY),
            lax.rem(z + dz + NZ, NZ),
            lax.rem(c + dc, 2),
        )

    used_s, used_r, sends = [0], [0], []

    def send_sem(ref):
        n = used_s[0]
        used_s[0] = n + 1
        sends.append((ssem.at[n], ref))
        return ssem.at[n]

    def recv_sem():
        n = used_r[0]
        used_r[0] = n + 1
        return rsem.at[n]

    def await_bytes(sem, ref):
        pltpu.make_async_copy(ref, ref, sem).wait()

    def copy(src, dst, at, s_sem, r_sem):
        pltpu.make_async_remote_copy(
            src_ref=src, dst_ref=dst, send_sem=s_sem, recv_sem=r_sem,
            device_id=device_of(*at), device_id_type=MESH,
        ).start()

    peers = [(0, 0, i, 0) for i in range(1, NZ)]
    peers += [(i, j, 0, 0) for i in range(NX) for j in range(NY) if i or j]
    peers += [(0, 0, i, 1) for i in range(NZ)]
    peers += [(0, j, 0, 1) for j in range(1, NY)]
    barrier = pltpu.get_barrier_semaphore()
    for p in peers:
        pl.semaphore_signal(barrier, inc=1, device_id=device_of(*near(*p)), device_id_type=MESH)

    h32 = h_ref[...].astype(F32)
    buf_a[x, c, y, z] = jnp.concatenate([h32[:, 0:256], h32[:, 256:512]], axis=0).astype(BF16)
    buf_b[x, c, y, z] = jnp.concatenate([h32[:, 512:768], h32[:, 768:1024]], axis=0).astype(BF16)
    pbuf[c, zl, x] = jnp.where(
        c == 0, pt_ref[:, 0:512].astype(F32), pt_ref[:, 512:1024].astype(F32)
    ).astype(BF16)
    loads = []
    for n, (src, dst) in enumerate(((wq_hbm, wq), (idx_hbm, idx), (slab_hbm, slab))):
        load = pltpu.make_async_copy(src, dst, local_sem.at[n])
        loads.append(load)
    loads[0].start()
    loads[1].start()

    owner = owner_ref[...]
    og, od = owner >> 4, owner & 15
    code = ((od & 3) * 4 + (og >> 2)) * 16 + (((og >> 1) & 1) * 4 + (od >> 2)) * 2 + (og & 1)
    sub, ln = iota((8, 128), 0), iota((8, 128), 1)
    count = jnp.zeros((8, 128), jnp.int32)
    for i in range(8):
        count = jnp.where(sub == i, count_ref[i], count)
    code = jnp.where(ln < count, code, -1).astype(F32)
    row = row_ref[...].astype(F32)
    high = jnp.floor(row * (1.0 / 16.0))
    low = row - 16.0 * high
    line = iota((128, 128), 0)
    kind, place = line % 16, line // 16
    upper = (line < iota((128, 128), 1)).astype(F32).astype(BF16)
    owner_line = iota((256, 128), 0).astype(F32)
    hits = [(code[i:i + 1] == owner_line).astype(F32) for i in range(8)]
    before = [jnp.dot(t.astype(BF16), upper, preferred_element_type=F32) for t in hits]
    totals = [jnp.sum(t, axis=1, keepdims=True) for t in hits]
    carry = jnp.zeros((256, 1), F32)
    table = jnp.zeros((256, 128), F32)
    for i in range(8):
        rank = jnp.sum(hits[i] * (before[i] + carry), axis=0, keepdims=True)
        carry = carry + totals[i]
        value = jnp.where(kind == 0, high[i:i + 1], jnp.where(kind == 1, low[i:i + 1], jnp.where(kind == 2, i + 1.0, 0.0)))
        value = jnp.where(rank == place.astype(F32), value, 0.0)
        table = table + nt(hits[i].astype(BF16), value.astype(BF16))
    tab[...] = table.astype(BF16).reshape(16, 16, 128)
    pl.semaphore_wait(barrier, len(peers))

    bufs = (buf_a, buf_b)
    z_sem = []
    for buf in bufs:
        s, r = send_sem(buf.at[0, 0, 0, 0:7]), recv_sem()
        for o in range(1, NZ):
            copy(buf.at[x, c, y, z], buf.at[x, c, y, z], near(0, 0, o, 0), s, r)
        z_sem.append(r)
    s, px_sem = send_sem(pbuf.at[0, 0, 0:3]), recv_sem()
    for o in range(1, NX):
        copy(pbuf.at[c, zl, x], pbuf.at[c, zl, x], near(o, 0, 0, 0), s, px_sem)

    spot = x * 4 + y
    s, ty_sem = send_sem(tab_y.at[0:15]), recv_sem()
    for i in range(NX):
        for j in range(NY):
            if i or j:
                to = near(i, j, 0, 0)
                copy(tab.at[to[0] * 4 + to[1]], tab_y.at[spot], to, s, ty_sem)
    tab_y[spot] = tab[spot]

    loads[2].start()

    loads[0].wait()
    q_own = jnp.dot(h_ref[...], wq[...], preferred_element_type=F32)
    rq_own = lax.rsqrt(jnp.mean(q_own * q_own, axis=1, keepdims=True) + EPS)
    u_own = q_own * rq_own
    pos = pos_ref[...].astype(F32)
    pos = pos * lax.rsqrt(jnp.mean(pos * pos, axis=1, keepdims=True) + EPS)
    pos_dot = jnp.sum(u_own * pos, axis=1, keepdims=True)
    pos_score = pos_dot * SCALE
    pos_exp = jnp.exp(pos_score)
    pos_dir = (pos - u_own * (pos_dot * (1.0 / E))) * (rq_own * SCALE)
    for k in range(2):
        posd[k] = pos_dir[:, k * 384:(k + 1) * 384]
    s, posd_sem = send_sem(posd.at[0]), recv_sem()
    copy(posd.at[1 - c], posd_in, near(0, 0, 0, 1), s, posd_sem)

    def along_x(o):
        return (o, 0, 0, 0)

    def along_y(o):
        return (0, o, 0, 0)

    mid_axis, last_axis = (along_y, along_x), (along_x, along_y)
    mid_sem, near_sem, far_sem, core_sem = [], [], [], []
    s_mid, s_near, s_far, s_core = [], [], [], []
    for buf in bufs:
        mid_sem.append([recv_sem() for _ in range(3)])
        near_sem.append([recv_sem() for _ in range(4)])
        far_sem.append(recv_sem())
        core_sem.append(recv_sem())
        s_mid.append(send_sem(buf.at[0, 0, 0:3]))
        s_near.append(send_sem(buf.at[:, 0, 0:2]))
        s_far.append(send_sem(buf.at[:, 0, 0]))
        s_core.append(send_sem(buf.at[:, 0]))

    def group(n, j, q):
        if n == 0:
            return buf_a.at[lax.rem(x - q + NX, NX), c, lax.rem(y - j + NY, NY)]
        return buf_b.at[lax.rem(x - j + NX, NX), c, lax.rem(y - q + NY, NY)]

    def to_core(n, ref):
        copy(ref, ref, near(0, 0, 0, 1), s_core[n], core_sem[n])

    def to_near(n, j):
        ref = group(n, j, 0)
        for o in (1, 3):
            copy(ref, ref, near(*last_axis[n](o)), s_near[n], near_sem[n][j])
        to_core(n, ref)

    def forward(n, j):
        await_bytes(near_sem[n][j], bufs[n].at[0, 0, 0:2])
        ahead, behind = group(n, j, 1), group(n, j, 3)
        lo, hi = ahead.at[0:4], behind.at[4:8]
        copy(lo, lo, near(*last_axis[n](1)), s_far[n], far_sem[n])
        copy(hi, hi, near(*last_axis[n](3)), s_far[n], far_sem[n])
        to_core(n, ahead)
        to_core(n, behind)

    for n, buf in enumerate(bufs):
        await_bytes(z_sem[n], buf.at[0, 0, 0, 0:7])
        ref = group(n, 0, 0)
        for o in range(1, 4):
            copy(ref, ref, near(*mid_axis[n](o)), s_mid[n], mid_sem[n][o - 1])
        to_near(n, 0)

    await_bytes(ty_sem, tab_y.at[0:15])
    tab_j[...] = jnp.swapaxes(tab_y[...].astype(F32), 0, 1).astype(BF16)
    s, tj_sem = send_sem(tab_r.at[0:15]), recv_sem()
    for o in range(NZ):
        for k in range(2):
            if o or k:
                to = near(0, 0, o, k)
                copy(tab_j.at[to[2] * 2 + to[3]], tab_r.at[z * 2 + c], to, s, tj_sem)
    tab_r[z * 2 + c] = tab_j[z * 2 + c]

    await_bytes(px_sem, pbuf.at[0, 0, 0:3])
    s, pz_sem = send_sem(pbuf.at[0, 0:3]), recv_sem()
    for o in (1, 7):
        copy(pbuf.at[c, zl], pbuf.at[c, zl], near(0, 0, o, 0), s, pz_sem)
    copy(pbuf.at[c, zl, 0:2], pbuf.at[c, zl, 0:2], near(0, 0, 2, 0), s, pz_sem)
    copy(pbuf.at[c, zl, 2:4], pbuf.at[c, zl, 2:4], near(0, 0, 6, 0), s, pz_sem)

    def middle(o):
        for n in range(2):
            await_bytes(mid_sem[n][o - 1], bufs[n].at[0, 0, 0])
            to_near(n, o)

    middle(1)
    middle(3)

    loads[1].wait()
    await_bytes(tj_sem, tab_r.at[0:15])
    src, out = iota((128, 2048), 0), iota((128, 2048), 1)
    slot, want_q = out // 256, (out // 128) % 2
    weight = jnp.where(src % 16 == 0, 16.0, 1.0)
    kept = jnp.where(want_q == 0, jnp.where(src % 16 < 2, weight, 0.0), jnp.where(src % 16 == 2, 1.0, 0.0))
    expand = jnp.where(src // 16 == slot, kept, 0.0).astype(BF16)

    def columns_of(b):
        wide = jnp.dot(tab_r[2 * b:2 * b + 2].reshape(32, 128), expand, preferred_element_type=F32)
        row = jnp.concatenate([wide[:, k * 256:k * 256 + 128] for k in range(8)], axis=0)
        qry = jnp.concatenate([wide[:, k * 256 + 128:k * 256 + 256] for k in range(8)], axis=0)
        return row, qry

    lane_f = iota((256, 128), 1).astype(F32)

    def pick(b):
        row, qry = columns_of(b)
        hot = jnp.concatenate(
            [(row == lane_f + 128.0 * t).astype(F32).astype(BF16) for t in range(16)], axis=1
        )
        r = jnp.dot(hot, idx[...], preferred_element_type=F32)
        rows[b] = r.astype(BF16)
        rr = lax.rsqrt(jnp.mean(r * r, axis=1, keepdims=True) + EPS)
        norm[b, 0] = jnp.broadcast_to(rr, (256, 128))
        norm[b, 1] = qry

    def onward(j):
        for n in range(2):
            forward(n, j)

    pick(0)
    middle(2)
    pick(1)
    onward(0)
    pick(2)
    onward(1)
    pick(3)
    pick(4)
    onward(3)
    await_bytes(pz_sem, pbuf.at[0, 0:3])
    s, pc_sem = send_sem(pbuf.at[0]), recv_sem()
    copy(pbuf.at[c], pbuf.at[c], near(0, 0, 0, 1), s, pc_sem)
    pick(5)
    onward(2)
    pick(6)
    pick(7)
    for n, buf in enumerate(bufs):
        await_bytes(far_sem[n], buf.at[:, 0, 0])
        for j in range(4):
            to_core(n, group(n, j, 2))
    for n, buf in enumerate(bufs):
        await_bytes(core_sem[n], buf.at[:, 0])

    def project(b, _):
        sides = []
        for buf in bufs:
            part = jnp.swapaxes(buf[:, :, :, b], 0, 1).astype(F32).reshape(32, 16, 256)
            sides += [part[:, 0:8].reshape(256, 256), part[:, 8:16].reshape(256, 256)]
        sides = [t.astype(BF16) for t in sides]
        for n, t in enumerate(sides):
            h_t[pl.ds(n * 256, 256), pl.ds(pl.multiple_of(b * 256, 256), 256)] = t.T
        q = jnp.dot(jnp.concatenate(sides, axis=1), wq[...], preferred_element_type=F32)
        rq = lax.rsqrt(jnp.mean(q * q, axis=1, keepdims=True) + EPS)
        u = q * rq
        hi = u.astype(BF16)
        u_two[b, 0:256] = hi
        u_two[b, 256:512] = (u - hi.astype(F32)).astype(BF16)
        u_scale[b] = jnp.broadcast_to(rq * SCALE, (256, 128))
        return 0

    lax.fori_loop(0, 8, project, 0, unroll=4)

    group_of = (iota((256, 256), 0) % 32 * 8 - 1).astype(F32)
    query_lane = iota((256, 256), 1).astype(F32)

    def score(b, _):
        r = rows[b]
        two = u_two[b]
        rr = norm[b, 0][:, 0:1]
        s = nt(two, r)
        s = (s[0:256] + s[256:512]).T * (rr * SCALE)
        qry = jnp.concatenate([norm[b, 1], norm[b, 1]], axis=1)
        live = (qry > 0.5) & (group_of + qry == query_lane)
        e = jnp.where(live, jnp.exp(s), 0.0)
        zr = jnp.sum(e, axis=0, keepdims=True)
        zbuf[b // 4, pl.ds(lax.rem(b, 4) * 2, 1), :] = zr[:, 0:128]
        zbuf[b // 4, pl.ds(lax.rem(b, 4) * 2 + 1, 1), :] = zr[:, 128:256]
        gb = tn((e * rr).astype(BF16), r)
        u = two[0:256].astype(F32) + two[256:512].astype(F32)
        gb = gb - u * (jnp.sum(u * gb, axis=1, keepdims=True) * (1.0 / E))
        gb = gb * u_scale[b][:, 0:1]
        at = pl.ds(pl.multiple_of(b * 256, 256), 256)
        ghat[0, at, :] = gb[:, 0:384]
        ghat[1, at, :] = gb[:, 384:768]
        return 0

    own_at = ((z * 2 + c) * 16 + x * 4 + y) * 8
    mine = jnp.sum(jnp.where(ln == lax.rem(own_at, 128) + sub, pos_exp, 0.0), axis=0, keepdims=True)
    z_sems = []

    def sums_core(k):
        zbuf[k] = zbuf[k] + jnp.where(sub + 8 * k == own_at // 128, mine, 0.0)
        s, r = send_sem(zrecv.at[k, 0]), recv_sem()
        copy(zbuf.at[k], zrecv.at[k, 0], near(0, 0, 0, 1), s, r)
        z_sems.append(r)

    def sums_xy(k):
        await_bytes(z_sems[k], zrecv.at[k, 0])
        zsum[k, 0] = zbuf[k] + zrecv[k, 0]
        s, r = send_sem(zrecv.at[k, 1:16]), recv_sem()
        n = 1
        for i in range(NX):
            for j in range(NY):
                if i or j:
                    copy(zsum.at[k, 0], zrecv.at[k, n], near(i, j, 0, 0), s, r)
                    n += 1
        return r

    def sums_z(k, r):
        await_bytes(r, zrecv.at[k, 1:16])
        total = zsum[k, 0]
        for n in range(1, 16):
            total = total + zrecv[k, n]
        zsum[k, 1] = total
        s, r = send_sem(zrecv.at[k, 16:23]), recv_sem()
        for o in range(1, NZ):
            copy(zsum.at[k, 1], zrecv.at[k, 15 + o], near(0, 0, o, 0), s, r)
        return r

    def sums_done(k, r):
        await_bytes(r, zrecv.at[k, 16:23])
        total = zsum[k, 1]
        for n in range(16, 23):
            total = total + zrecv[k, n]
        turned = jnp.concatenate([total, jnp.ones((120, 128), F32)], axis=0).T
        for t in range(8):
            zcol[pl.ds(k * 1024 + t * 128, 128), :] = jnp.broadcast_to(
                turned[:, t:t + 1], (128, 128)
            )

    def encode(lo, hi):
        def step(n, _):
            at = pl.ds(pl.multiple_of(n * 256, 256), 256)
            t = slab[at, :]
            q0, q1 = pbuf[0].reshape(E, 512), pbuf[1].reshape(E, 512)
            ren[at, :] = (nt(t[:, 0:512], q0) + nt(t[:, 512:1024], q1)).astype(BF16)
            return 0

        lax.fori_loop(lo, hi, step, 0)

    own = pl.ds(pl.multiple_of(own_at, 8), 8)
    partner = pl.ds(pl.multiple_of(((z * 2 + 1 - c) * 16 + x * 4 + y) * 8, 8), 8)
    g_sems = []

    def terms_core(k):
        @pl.when(own_at // 1024 == k)
        def _():
            for t in range(2):
                ghat[t, own, :] = ghat[t, own, :] + posd[t] * pos_exp

        span = pl.ds(k * 1024, 1024)
        s, r = send_sem(gother.at[span]), recv_sem()
        copy(ghat.at[1 - c, span], gother.at[span], near(0, 0, 0, 1), s, r)
        g_sems.append(r)

    def rescale(k):
        await_bytes(g_sems[k], gother.at[pl.ds(k * 1024, 1024)])

        @pl.when(own_at // 1024 == k)
        def _():
            ghat[c, own, :] = ghat[c, own, :] - posd[c] * zcol[own, :][:, 0:1]
            ghat[c, partner, :] = ghat[c, partner, :] - posd_in[...] * zcol[partner, :][:, 0:1]

        def step(b, _):
            at = pl.ds(pl.multiple_of(b * 128, 128), 128)
            gmat[at, :] = ((ghat[c, at, :] + gother[at, :]) / zcol[at, :][:, 0:1]).astype(BF16)
            return 0

        lax.fori_loop(k * 8, k * 8 + 8, step, 0, unroll=4)

    unit_x = [1, 1 - c, 0]
    first_at = [x * f + y * (1 - f) for f in unit_x]
    second_at = [y * f + x * (1 - f) for f in unit_x]
    quarter = [lax.rem(zl + 1 + n, 4) for n in range(4)]

    def product(n, k):
        at = pl.ds(pl.multiple_of(quarter[n] * 256, 256), 256)
        span = pl.ds(k * 1024, 1024)
        return jnp.dot(h_t[at, span], gmat[span, :], preferred_element_type=F32)

    def keep(n, val, more):
        for u in range(3):
            tile = val[:, u * 128:(u + 1) * 128].reshape(4, 4, 16, 128)
            if u == 0:
                tt[n, u] = tt[n, u] + tile if more else tile
                continue
            for i in range(4):
                for j in range(4):
                    a = i * unit_x[u] + j * (1 - unit_x[u])
                    b = j * unit_x[u] + i * (1 - unit_x[u])
                    part = tile[i, j]
                    tt[n, u, a, b] = tt[n, u, a, b] + part if more else part

    lax.fori_loop(0, 4, score, 0, unroll=4)
    sums_core(0)
    terms_core(0)
    lax.fori_loop(4, 6, score, 0, unroll=2)
    xy_0 = sums_xy(0)
    lax.fori_loop(6, 8, score, 0, unroll=2)
    sums_core(1)
    terms_core(1)
    za_0 = sums_z(0, xy_0)
    loads[2].wait()
    await_bytes(pc_sem, pbuf.at[0])
    encode(0, 1)
    xy_1 = sums_xy(1)
    encode(1, 3)
    sums_done(0, za_0)
    await_bytes(posd_sem, posd_in)
    rescale(0)
    za_1 = sums_z(1, xy_1)
    for n in range(4):
        keep(n, product(n, 0), False)
    encode(3, 4)
    sums_done(1, za_1)
    rescale(1)

    z_own = zcol[own, :][:, 0:1]
    loss = jnp.log(z_own) - pos_score
    loss_ref[...] = jnp.sum(jnp.where(sub == ln, loss, 0.0), axis=0, keepdims=True)[:, 0:8]
    pair_rows = jnp.concatenate(
        [(ghat[c, at, :] + gother[at, :]) / zcol[at, :][:, 0:1] for at in (own, partner)], axis=0
    )
    pair_low = (pair_rows - pair_rows.astype(BF16).astype(F32)).astype(BF16)
    pair_h = []
    for buf in bufs:
        mine, its = buf[x, c, y, z].astype(F32), buf[x, 1 - c, y, z].astype(F32)
        for at in (slice(0, 8), slice(8, 16)):
            pair_h.append(jnp.concatenate([mine[at], its[at]], axis=0))

    s_r1, r1_sem = send_sem(r1), [recv_sem() for _ in range(4)]
    s_r2, r2_sem = send_sem(r2), [recv_sem() for _ in range(4)]
    s_r3, r3_sem = send_sem(r3), recv_sem()

    def produce(n):
        val = product(n, 1)
        mine = jnp.zeros((16, 256), F32)
        for t in range(4):
            mine = jnp.where(quarter[n] == t, pair_h[t], mine)
        val = val + tn(mine.astype(BF16), pair_low)
        keep(n, val, True)

    def step_first(n):
        for u in range(3):
            f = unit_x[u]
            for o in range(1, 4):
                to = lax.rem(first_at[u] + o, 4)
                copy(
                    tt.at[n, u, to], r1.at[n, u, o - 1], near(o * f, o * (1 - f), 0, 0),
                    s_r1, r1_sem[n],
                )

    def step_second(n):
        await_bytes(r1_sem[n], r1.at[n])
        for u in range(3):
            f = unit_x[u]
            p1[n, u] = tt[n, u, first_at[u]] + (r1[n, u, 0] + r1[n, u, 1] + r1[n, u, 2])
            for o in range(1, 4):
                to = lax.rem(second_at[u] + o, 4)
                copy(
                    p1.at[n, u, to], r2.at[n, u, o - 1], near(o * (1 - f), o * f, 0, 0),
                    s_r2, r2_sem[n],
                )

    def step_z(n):
        await_bytes(r2_sem[n], r2.at[n])
        for u in range(3):
            p2[n, u] = p1[n, u, second_at[u]] + (r2[n, u, 0] + r2[n, u, 1] + r2[n, u, 2])
        for k in range(2):
            if n < 3 or k:
                to = lax.rem(zl + n + 1, 4) + 4 * k
                if n == 3:
                    to = lax.rem(z + 4, 8)
                away = lax.rem(to - z + NZ, NZ)
                copy(p2.at[n], r3.at[away - 1], (x, y, to, c), s_r3, r3_sem)

    for n in range(4):
        produce(n)
        step_first(n)
    encode(4, 5)
    step_second(0)
    encode(5, 6)
    step_second(1)
    step_z(0)
    encode(6, 7)
    step_second(2)
    step_z(1)
    encode(7, 8)
    out_copy = pltpu.make_async_copy(ren, ren_hbm, local_sem.at[3])
    out_copy.start()
    step_second(3)
    step_z(2)
    step_z(3)
    await_bytes(r3_sem, r3)
    done = p2[3]
    for o in range(NZ - 1):
        done = done + r3[o]
    at = y * 2 + c
    fin[at] = done
    s, r = send_sem(fin.at[0:7]), recv_sem()
    for o in range(NY):
        for k in range(2):
            if o or k:
                copy(fin.at[at], fin.at[at], near(0, o, 0, k), s, r)
    await_bytes(r, fin.at[0:7])
    for j in range(NY):
        for n in range(2):
            for u in range(3):
                grad_ref[pl.ds(j * 16, 16), pl.ds(n * 384 + u * 128, 128)] = fin[j * 2 + n, u]
    for sem, ref in sends:
        await_bytes(sem, ref)
    out_copy.wait()
    assert (used_s[0], used_r[0]) == (SENDS, RECVS)


def hand_over(loss_in, grad_in, ren_in, loss_out, grad_out, ren_out, held, sem):
    parts = 4
    size = ren_in.shape[0] // parts
    ins, outs = [], []
    for n in range(parts):
        at = pl.ds(n * size, size)
        ins.append(pltpu.make_async_copy(ren_in.at[at], held.at[at], sem.at[n]))
        outs.append(pltpu.make_async_copy(held.at[at], ren_out.at[at], sem.at[parts + n]))
    for copy in ins:
        copy.start()
    loss_out[...] = loss_in[...]
    grad_out[...] = grad_in[...]
    for first, then in zip(ins, outs):
        first.wait()
        then.start()
    for copy in outs:
        copy.wait()


SENDS = 28
RECVS = 44


def local(
    question_encoder_states,
    query_proj,
    positive_embed,
    stale_index,
    neg_owner,
    neg_row,
    neg_count,
    slab_hidden,
    passage_projector,
):
    vmem = pl.BlockSpec(memory_space=pltpu.VMEM)
    smem = pl.BlockSpec(memory_space=pltpu.SMEM)
    hbm = pl.BlockSpec(memory_space=pl.ANY)
    V = pltpu.VMEM
    scratch = [
        V((D, E), BF16), V((2048, E), BF16), V((2048, D), BF16), V((2048, E), BF16),
        pltpu.SemaphoreType.DMA((4,)),
        V((NX, 2, NY, NZ, 16, 256), BF16), V((NX, 2, NY, NZ, 16, 256), BF16),
        V((D, 2048), BF16),
        V((16, 16, 128), BF16), V((16, 16, 128), BF16), V((16, 16, 128), BF16),
        V((16, 16, 128), BF16),
        V((2, 4, 4, 48, 512), BF16), V((8, 256, E), BF16), V((8, 2, 256, 128), F32),
        V((8, 512, E), BF16), V((8, 256, 128), F32),
        V((2, 2048, 384), F32), V((2048, 384), F32), V((2, 8, 384), F32), V((8, 384), F32),
        V((2048, 384), BF16),
        V((2, 8, 128), F32), V((2, 23, 8, 128), F32), V((2, 2, 8, 128), F32), V((2048, 128), F32),
        V((4, 3, 4, 4, 16, 128), F32),
        V((4, 3, 3, 4, 16, 128), F32), V((4, 3, 4, 16, 128), F32),
        V((4, 3, 3, 16, 128), F32), V((4, 3, 16, 128), F32),
        V((NZ - 1, 3, 16, 128), F32), V((NY * 2, 3, 16, 128), F32),
        pltpu.SemaphoreType.DMA((SENDS,)), pltpu.SemaphoreType.DMA((RECVS,)),
    ]
    shapes = (
        jax.ShapeDtypeStruct((1, 8), F32),
        jax.ShapeDtypeStruct((64, E), F32),
        jax.ShapeDtypeStruct((2048, E), BF16),
    )
    results = pl.pallas_call(
        body,
        out_shape=shapes,
        in_specs=[vmem, vmem, vmem, smem, vmem, vmem, hbm, hbm, hbm],
        out_specs=(vmem, vmem, hbm),
        scratch_shapes=scratch,
        compiler_params=pltpu.CompilerParams(
            collective_id=0, has_side_effects=True, vmem_limit_bytes=62 * 2**20
        ),
        cost_estimate=pl.CostEstimate(
            flops=30 * 10**9, bytes_accessed=16 * 2**20, transcendentals=2**20
        ),
    )(
        question_encoder_states, neg_owner[..., 0], neg_row, neg_count, positive_embed,
        passage_projector.T, query_proj, stale_index, slab_hidden,
    )
    losses, grad, renewed = pl.pallas_call(
        hand_over,
        out_shape=shapes,
        in_specs=[vmem, vmem, hbm],
        out_specs=(vmem, vmem, hbm),
        scratch_shapes=[V((2048, E), BF16), pltpu.SemaphoreType.DMA((8,))],
        compiler_params=pltpu.CompilerParams(vmem_limit_bytes=62 * 2**20),
    )(*results)
    return losses.reshape(8), grad, renewed


def solution(mesh):
    rows = P(("group", "dev"), None)
    in_specs = (
        rows, P(), rows, rows, P(("group", "dev"), None, None), rows,
        P(("group", "dev")), rows, P(None, "dev"),
    )
    out_specs = (P(("group", "dev")), P("dev", None), rows)
    return jax.shard_map(local, mesh=mesh, in_specs=in_specs, out_specs=out_specs, check_vma=False)
```
